32 devices in a mesh: aperture: 16 (over z, x, core), tile: 2 (over y).
Axes of the slice: x: 2, y: 2, z: 4, core: 2. Of those that a mesh axis runs over, the one named last changes fastest.
Arguments:
- raw_echoes: bfloat16 [2, 2048, 2048], P(None, 'aperture', 'tile'), may hold values from -6 to 6
- chirp_taps: bfloat16 [2, 256], replicated, may hold values from -0.25 to 0.25
- steering: bfloat16 [2, 64, 160], replicated, may hold values from -0.3125 to 0.3125
- offsets: int32 [2, 2, 128], replicated, may hold values from 0 to 56
- band_coef: float32 [2, 2, 128, 8], replicated, may hold values from -2.5 to 2.5
- phase_slope: float32 [2, 2, 128], replicated, may hold values from -40 to 40
- phase_base: float32 [2, 2, 128], replicated, may hold values from -3.140625 to 3.140625
Outputs:
- image: float32 [2, 1024, 2048], P(None, 'aperture', 'tile')
The draws below stay inside these ranges and needn't reach their ends.
Inputs may be any that keep to these rules, and one draw needn't show every extreme that they name: `offsets`: the first input beam of each 8-tap band, so that the band lies within the 64 input beams.
All inputs are finite; a program needn't handle non-finite values.
Results may differ from the reference program's by a relative error of at most 0.0029.
Values may be sent and summed in bfloat16 or wider, within the bound.
No kernel may reach another device: no remote copies, remote signals or barrier semaphores. Data moves between devices by JAX's collectives and lax.ppermute only.
A program may use at most 64 MiB of HBM per device.

```python
import jax
import jax.numpy as jnp
from jax import lax

P_DEV = 128
GUARD = 32
TAPS = 256
BEAMS = 64
INTERP = 8
PULSES = 2048
RANGE = 2048
N_APERTURE = 16


def set_ends(array, stream_key, smallest, largest):
    longest = array.shape.index(max(array.shape))
    spots = []
    for shift in (0, 1):
        where = [jax.random.randint(jax.random.fold_in(stream_key, axis), (), 0, length) for axis, length in enumerate(array.shape)]
        where[longest] = (where[longest] + shift) % array.shape[longest]
        spots.append(tuple(where))
    return array.at[spots[0]].set(smallest).at[spots[1]].set(largest)


def shard_levels(own_key, shape, cuts, smallest, high):
    def one(dim, shards_of):
        draws = jax.random.uniform(jax.random.fold_in(jax.random.fold_in(own_key, 6), dim), (shards_of,), jnp.float32, smallest / len(cuts), high / len(cuts))
        return jnp.repeat(jnp.exp(draws), shape[dim] // shards_of).reshape((-1,) + (1,) * (len(shape) - dim - 1))

    level = one(*cuts[0])
    for cut in cuts[1:]:
        level = level * one(*cut)
    return level


def noise(key, extent, width, limit, split=(), held_as=jnp.bfloat16):
    drawn = width * jax.random.normal(key, extent, jnp.float32)
    if split:
        drawn = drawn * shard_levels(key, extent, split, -0.22, 0.18)
    return jnp.clip(drawn, -limit, limit).astype(held_as)


def setup_inputs(seed: int = 0) -> dict:
    seeds = jax.random.split(jax.random.key(seed), 8)
    return {
        "raw_echoes": noise(seeds[0], (2, PULSES, RANGE), 1.0, 6.0, ((1, 16), (2, 2))),
        "chirp_taps": noise(seeds[1], (2, TAPS), (2 * TAPS) ** -0.5, 0.25),
        "steering": noise(seeds[2], (2, BEAMS, P_DEV + GUARD), (2 * (P_DEV + GUARD)) ** -0.5, 0.3125),
        "offsets": set_ends(jax.random.randint(seeds[3], (2, 2, 2 * BEAMS), 0, BEAMS - INTERP + 1), jax.random.fold_in(seeds[3], 1), 0, BEAMS - INTERP).astype(jnp.int32),
        "band_coef": noise(seeds[4], (2, 2, 2 * BEAMS, INTERP), 0.35, 2.5, (), jnp.float32),
        "phase_slope": jnp.clip(jax.random.uniform(seeds[5], (2, 2, 2 * BEAMS), jnp.float32, -40.0, 40.0), -40.0, 40.0),
        "phase_base": jnp.clip(jax.random.uniform(seeds[6], (2, 2, 2 * BEAMS), jnp.float32, -3.140625, 3.140625), -3.140625, 3.140625),
    }


def chirp_matrix(chirp_taps):
    tap_count = chirp_taps.shape[1]
    row_idx = jnp.arange(tap_count, dtype=jnp.int32)[:, None]
    col_idx = jnp.arange(tap_count, dtype=jnp.int32)[None, :]
    nought = jnp.zeros((), chirp_taps.dtype)
    near_lag = row_idx - col_idx
    far_lag = row_idx - col_idx + tap_count

    def toeplitz(tap_values):
        near_block = jnp.where(near_lag >= 0, jnp.take(tap_values, jnp.clip(near_lag, 0, tap_count - 1)), nought)
        far_block = jnp.where(far_lag < tap_count, jnp.take(tap_values, jnp.clip(far_lag, 0, tap_count - 1)), nought)
        return near_block, far_block

    near_re, far_re = toeplitz(chirp_taps[0])
    near_im, far_im = toeplitz(chirp_taps[1])
    return jnp.concatenate([
        jnp.concatenate([near_re, -near_im], 1),
        jnp.concatenate([near_im, near_re], 1),
        jnp.concatenate([far_re, -far_im], 1),
        jnp.concatenate([far_im, far_re], 1)], 0)


def compress(echoes, rim_part, weight):
    tap_count = rim_part.shape[2]
    pulse_count = echoes.shape[1]
    bin_count = echoes.shape[2]
    blocks = bin_count // tap_count
    extended = jnp.concatenate([echoes, rim_part], 2).reshape(2, pulse_count, blocks + 1, tap_count)
    features = jnp.concatenate([extended[0, :, :blocks], extended[1, :, :blocks],
                                extended[0, :, 1:], extended[1, :, 1:]], 2)
    result = jnp.dot(features.reshape(pulse_count * blocks, 4 * tap_count), weight,
                     preferred_element_type=jnp.float32)
    result = result.reshape(pulse_count, blocks, 2 * tap_count)
    real_part = result[:, :, :tap_count].reshape(pulse_count, bin_count)
    imag_part = result[:, :, tap_count:].reshape(pulse_count, bin_count)
    return jnp.stack([real_part, imag_part]).astype(jnp.bfloat16)


def beamform(steering, compressed):
    real_part = (jnp.dot(steering[0], compressed[0], preferred_element_type=jnp.float32)
                 - jnp.dot(steering[1], compressed[1], preferred_element_type=jnp.float32))
    imag_part = (jnp.dot(steering[0], compressed[1], preferred_element_type=jnp.float32)
                 + jnp.dot(steering[1], compressed[0], preferred_element_type=jnp.float32))
    return jnp.stack([real_part, imag_part])


def band_matrix(starts, weights, col_count):
    columns = jnp.arange(col_count, dtype=jnp.int32)
    taps_idx = jnp.arange(weights.shape[1], dtype=jnp.int32)
    selected = columns[None, None, :] == (starts[:, None] + taps_idx[None, :])[:, :, None]
    return jnp.sum(jnp.where(selected, weights[:, :, None], jnp.zeros((), weights.dtype)), axis=1)


def steered_term(starts, weights, slopes, phase_bases, source, position):
    matrix = band_matrix(starts, weights, source.shape[1])
    real_in = jnp.dot(matrix, source[0], precision=lax.Precision.HIGHEST, preferred_element_type=jnp.float32)
    imag_in = jnp.dot(matrix, source[1], precision=lax.Precision.HIGHEST, preferred_element_type=jnp.float32)
    phase_angle = slopes[:, None] * position[None, :] + phase_bases[:, None]
    cosine = jnp.cos(phase_angle)
    sine_part = jnp.sin(phase_angle)
    return jnp.stack([cosine * real_in - sine_part * imag_in, sine_part * real_in + cosine * imag_in])


def side_rows(param_tables, section_no, side_no, start_row, row_count):
    picked = []
    for param_table in param_tables:
        layer = lax.dynamic_index_in_dim(param_table[section_no], side_no, 0, keepdims=False)
        picked.append(lax.dynamic_slice_in_dim(layer, start_row, row_count, 0))
    return picked


def reference(raw_echoes, chirp_taps, steering, offsets, band_coef, phase_slope, phase_base):
    weight = chirp_matrix(chirp_taps)
    padded = jnp.concatenate([raw_echoes, jnp.zeros((2, GUARD, RANGE), raw_echoes.dtype)], 1)
    empty_rim = jnp.zeros((2, P_DEV + GUARD, TAPS), raw_echoes.dtype)

    def one_block(device):
        echoes = lax.dynamic_slice_in_dim(padded, device * P_DEV, P_DEV + GUARD, 1)
        return beamform(steering, compress(echoes, empty_rim, weight))

    devices = jnp.arange(N_APERTURE, dtype=jnp.int32)
    subimages = lax.map(one_block, devices)
    position = jnp.arange(RANGE, dtype=jnp.int32).astype(jnp.float32) / float(RANGE)
    tables = (offsets, band_coef, phase_slope, phase_base)
    top_bit = N_APERTURE.bit_length() - 1
    for section_no in range(2):
        level_bit = top_bit - 2 + section_no
        distance = 1 << level_bit

        def merge_one(device, subimages=subimages, section_no=section_no, level_bit=level_bit, distance=distance):
            upper_half = (device >> level_bit) & 1
            lower_idx = device - upper_half * distance
            start_row = upper_half * BEAMS
            low_sub = lax.dynamic_index_in_dim(subimages, lower_idx, 0, keepdims=False)
            high_sub = lax.dynamic_index_in_dim(subimages, lower_idx + distance, 0, keepdims=False)
            low_term = steered_term(*side_rows(tables, section_no, 0, start_row, BEAMS), low_sub, position)
            high_term = steered_term(*side_rows(tables, section_no, 1, start_row, BEAMS), high_sub, position)
            return low_term + high_term

        subimages = lax.map(merge_one, devices)
    return jnp.transpose(subimages, (1, 0, 2, 3)).reshape(2, N_APERTURE * BEAMS, RANGE)
```

```python
import functools

import jax
import jax.numpy as jnp
from jax import lax
from jax.experimental import pallas as pl
from jax.experimental.pallas import tpu as pltpu
from jax.sharding import PartitionSpec as P

LANES = 128
VMEM = pltpu.CompilerParams(vmem_limit_bytes=24 * 1024 * 1024)


def call(body, outs, args, scratch=(), flops=0, aliases=None, in_specs=None, out_specs=None):
    whole = pl.BlockSpec(memory_space=pltpu.VMEM)
    many = isinstance(outs, (list, tuple))
    moved = sum(a.size * a.dtype.itemsize for a in list(args) + (list(outs) if many else [outs]))
    return pl.pallas_call(
        body,
        out_shape=outs,
        in_specs=in_specs or [whole] * len(args),
        out_specs=out_specs or ([whole] * len(outs) if many else whole),
        scratch_shapes=list(scratch),
        input_output_aliases=aliases or {},
        compiler_params=VMEM,
        cost_estimate=pl.CostEstimate(flops=flops, bytes_accessed=moved, transcendentals=0),
    )(*args)


def toeplitz_kernel(taps_ref, w_ref):
    count = taps_ref.shape[1]
    halves = []
    for part in range(2):
        row = taps_ref[part : part + 1, :].astype(jnp.float32)
        row = jnp.concatenate([row, jnp.zeros_like(row)], 1)
        rows = jnp.broadcast_to(row, (count, 2 * count))
        rolled = pltpu.roll(rows, 0, 1, stride=1, stride_axis=0)
        halves.append(rolled.T)
    for side in range(2):
        re = halves[0][side * count : (side + 1) * count].astype(jnp.bfloat16)
        im = halves[1][side * count : (side + 1) * count].astype(jnp.bfloat16)
        w_ref[side, :count, :count] = re
        w_ref[side, :count, count:] = -im
        w_ref[side, count:, :count] = im
        w_ref[side, count:, count:] = re


def split(value):
    high = value.astype(jnp.bfloat16)
    low = (value - high.astype(jnp.float32)).astype(jnp.bfloat16)
    return high, low


def table_kernel(level, offsets_ref, coef_ref, slope_ref, base_ref, m_ref, e_ref, turned):
    beams = e_ref.shape[3]
    bins = e_ref.shape[4]
    taps = coef_ref.shape[2]
    device = lax.axis_index("aperture")
    tile = lax.axis_index("tile")
    total = bins * lax.axis_size("tile")
    fine_bin = lax.broadcasted_iota(jnp.int32, (beams, LANES), 1)
    coarse_bin = fine_bin * LANES + tile * bins
    for s in range(2):
        upper = (device >> (level + s)) & 1
        start = pl.multiple_of(upper * beams, beams)
        for q in range(2):
            side = jnp.where(upper == q, 0, 1)
            rows = lax.broadcasted_iota(jnp.int32, (beams, 2 * beams), 0)
            lag = rows - offsets_ref[s, q : q + 1, :]
            matrix = jnp.zeros((beams, 2 * beams), jnp.float32)
            for t in range(taps):
                matrix += jnp.where(lag == t, coef_ref[s, q, t : t + 1, :], 0.0)
            pad = jnp.zeros((beams - 2, 2 * beams), jnp.float32)
            stacked = jnp.concatenate(
                [matrix, slope_ref[s, q : q + 1, :], base_ref[s, q : q + 1, :], pad], 0
            )
            turned[...] = stacked.T
            mine = turned[pl.ds(start, beams), :]
            high, low = split(mine[:, :beams])
            m_ref[s, side, :, :] = jnp.concatenate([high, low, high], 1)
            slope = mine[:, beams : beams + 1]
            base = mine[:, beams + 1 : beams + 2]
            fine = slope * (fine_bin.astype(jnp.float32) / float(total))
            coarse = slope * (coarse_bin.astype(jnp.float32) / float(total)) + base
            fine_cos, fine_sin = jnp.cos(fine), jnp.sin(fine)
            coarse_cos, coarse_sin = jnp.cos(coarse), jnp.sin(coarse)
            for k in range(bins // LANES):
                c, d = coarse_cos[:, k : k + 1], coarse_sin[:, k : k + 1]
                at = slice(k * LANES, (k + 1) * LANES)
                e_ref[s, side, 0, :, at] = c * fine_cos - d * fine_sin
                e_ref[s, side, 1, :, at] = d * fine_cos + c * fine_sin


def focus_kernel(first, has_rim, *refs):
    if has_rim:
        raw, guard, rim, corner, w, steering, high_ref, low_ref, x = refs
    else:
        raw, guard, w, steering, high_ref, low_ref, x = refs
    pulses, guards = raw.shape[1], guard.shape[1]
    width = w.shape[1] // 2
    rows = pulses + guards
    bins = high_ref.shape[2]
    blocks = bins // width
    for b in range(blocks + 1):
        at = first + b * width
        for part in range(2):
            lanes = slice(part * width, (part + 1) * width)
            if at < raw.shape[2]:
                own, other = raw[part, :, at : at + width], guard[part, :, at : at + width]
            else:
                own, other = rim[part], corner[part]
            x[b * rows : b * rows + pulses, lanes] = own
            x[b * rows + pulses : (b + 1) * rows, lanes] = other
    turned = jnp.concatenate([steering[0], steering[1]], 0)
    crossed = jnp.concatenate([-steering[1], steering[0]], 0)
    beams = steering.shape[1]
    out = jnp.dot(x[: blocks * rows], w[0], preferred_element_type=jnp.float32)
    out += jnp.dot(x[rows:], w[1], preferred_element_type=jnp.float32)
    out = out.astype(jnp.bfloat16)
    for b in range(blocks):
        re = out[b * rows : (b + 1) * rows, :width]
        im = out[b * rows : (b + 1) * rows, width:]
        sub = jnp.dot(turned, re, preferred_element_type=jnp.float32)
        sub += jnp.dot(crossed, im, preferred_element_type=jnp.float32)
        high, low = split(sub)
        at = slice(b * width, (b + 1) * width)
        high_ref[0, :, at], high_ref[1, :, at] = high[:beams], high[beams:]
        low_ref[0, :, at], low_ref[1, :, at] = low[:beams], low[beams:]


def merged(s, first, high, low, other, m, e):
    bins = high.shape[2]
    beams = high.shape[1]
    at = slice(first, first + bins)
    own_m = m[s, 0]
    other_m = m[s, 1][:, : 2 * beams]
    own, got = [], []
    for part in range(2):
        x = high[part]
        own.append(
            jnp.dot(own_m, jnp.concatenate([x, x, low[part]], 0), preferred_element_type=jnp.float32)
        )
        y = other[part]
        got.append(
            jnp.dot(other_m, jnp.concatenate([y, y], 0), preferred_element_type=jnp.float32)
        )
    c0, s0 = e[s, 0, 0, :, at], e[s, 0, 1, :, at]
    c1, s1 = e[s, 1, 0, :, at], e[s, 1, 1, :, at]
    re = c0 * own[0] - s0 * own[1] + c1 * got[0] - s1 * got[1]
    im = s0 * own[0] + c0 * own[1] + s1 * got[0] + c1 * got[1]
    return re, im


def first_merge_kernel(first, high, low, other, m, e, high_ref, low_ref):
    for part, value in enumerate(merged(0, first, high, low, other, m, e)):
        top, rest = split(value)
        high_ref[part] = top
        low_ref[part] = rest


def last_merge_kernel(first, high, low, other, m, e, *refs):
    image, held, sem = refs[-3:]
    for part, value in enumerate(merged(1, first, high, low, other, m, e)):
        held[part] = value
    copy = pltpu.make_async_copy(held, image.at[:, :, first : first + held.shape[2]], sem)
    copy.start()
    copy.wait()


def cut_kernel(raw, guard, rim, corner, sem):
    guards, width = corner.shape[1:]
    copies = [
        pltpu.make_async_copy(raw.at[:, :guards, :], guard, sem.at[0]),
        pltpu.make_async_copy(raw.at[:, :, :width], rim, sem.at[1]),
        pltpu.make_async_copy(raw.at[:, :guards, :width], corner, sem.at[2]),
    ]
    for copy in copies:
        copy.start()
    for copy in copies:
        copy.wait()


def shards(raw, taps, steering, offsets, coef, slope, base):
    pulses, bins = raw.shape[1:]
    width = taps.shape[1]
    beams = steering.shape[1]
    guards = steering.shape[2] - pulses
    count, tiles = lax.axis_size("aperture"), lax.axis_size("tile")
    level = count.bit_length() - 3
    bf16, f32 = jnp.bfloat16, jnp.float32
    sds = jax.ShapeDtypeStruct
    anywhere = pl.BlockSpec(memory_space=pl.ANY)
    whole = pl.BlockSpec(memory_space=pltpu.VMEM)

    guard, rim, corner = call(
        cut_kernel,
        [sds((2, guards, bins), bf16), sds((2, pulses, width), bf16), sds((2, guards, width), bf16)],
        [raw],
        scratch=[pltpu.SemaphoreType.DMA((3,))],
        in_specs=[anywhere],
        out_specs=[anywhere] * 3,
    )
    guard = lax.ppermute(guard, "aperture", [(d, d - 1) for d in range(1, count)])
    rim = lax.ppermute(rim, "tile", [(t, t - 1) for t in range(1, tiles)])
    corner = lax.ppermute(
        corner,
        ("aperture", "tile"),
        [
            (d * tiles + t, (d - 1) * tiles + t - 1)
            for d in range(1, count)
            for t in range(1, tiles)
        ],
    )
    w = call(toeplitz_kernel, sds((2, 2 * width, 2 * width), bf16), [taps])
    m, e = call(
        functools.partial(table_kernel, level),
        [sds((2, 2, beams, 3 * beams), bf16), sds((2, 2, 2, beams, bins), f32)],
        [offsets, jnp.swapaxes(coef, 2, 3), slope, base],
        scratch=[pltpu.VMEM((2 * beams, 2 * beams), f32)],
        flops=40_000_000,
    )

    half = bins // width // 2 * width
    chunks = [(0, half), (half, bins - half)] if half else [(0, bins)]

    def partner(value, bit):
        return lax.ppermute(value, "aperture", [(d, d ^ (1 << bit)) for d in range(count)])

    subs = []
    for first, size in chunks:
        has_rim = first + size == bins
        rows = pulses + guards
        args = [raw, guard] + ([rim, corner] if has_rim else []) + [w, steering]
        shape = sds((2, beams, size), bf16)
        subs.append(
            call(
                functools.partial(focus_kernel, first, has_rim),
                [shape, shape],
                args,
                scratch=[pltpu.VMEM(((size // width + 1) * rows, 2 * width), bf16)],
                flops=rows * size * 4 * width * 4,
            )
        )
    others = [partner(high, level) for high, _ in subs]
    seconds = []
    for (first, size), (high, low), other in zip(chunks, subs, others):
        shape = sds((2, beams, size), bf16)
        seconds.append(
            call(
                functools.partial(first_merge_kernel, first),
                [shape, shape],
                [high, low, other, m, e],
                flops=beams * size * beams * 40,
            )
        )
    others = [partner(high, level + 1) for high, _ in seconds]
    image = None
    for (first, size), (high, low), other in zip(chunks, seconds, others):
        args = [high, low, other, m, e] + ([] if image is None else [image])
        image = call(
            functools.partial(last_merge_kernel, first),
            sds((2, beams, bins), f32),
            args,
            scratch=[pltpu.VMEM((2, beams, size), f32), pltpu.SemaphoreType.DMA],
            aliases={} if image is None else {5: 0},
            in_specs=[whole] * 5 + ([] if image is None else [anywhere]),
            out_specs=anywhere,
            flops=beams * size * beams * 40,
        )
    return image


def solution(mesh):
    placed = (P(None, "aperture", "tile"), P(), P(), P(), P(), P(), P())
    return jax.shard_map(
        shards, mesh=mesh, in_specs=placed, out_specs=P(None, "aperture", "tile"), check_vma=False
    )
```

```python
import functools
import math

import jax
import jax.numpy as jnp
from jax import lax
from jax.experimental import pallas as pl
from jax.experimental.pallas import tpu as pltpu
from jax.sharding import PartitionSpec as P

LANES = 128
VMEM = pltpu.CompilerParams(vmem_limit_bytes=24 * 1024 * 1024)


def call(body, outs, args, scratch=(), flops=0, aliases=None, in_specs=None, out_specs=None, after=()):
    whole = pl.BlockSpec(memory_space=pltpu.VMEM)
    if after:
        inner, given, unused = body, len(args), len(after)
        in_specs = (in_specs or [whole] * given) + [pl.BlockSpec(memory_space=pl.ANY)] * unused
        args = list(args) + list(after)

        def body(*refs):
            inner(*refs[:given], *refs[given + unused :])

    many = isinstance(outs, (list, tuple))
    return pl.pallas_call(
        body,
        out_shape=outs,
        in_specs=in_specs or [whole] * len(args),
        out_specs=out_specs or ([whole] * len(outs) if many else whole),
        scratch_shapes=list(scratch),
        input_output_aliases=aliases or {},
        compiler_params=VMEM,
        cost_estimate=pl.CostEstimate(flops=flops, bytes_accessed=0, transcendentals=0),
    )(*args)


def completed(pairs, count):
    needed = dict(pairs)
    back = {t: s for s, t in needed.items() if t not in needed and s not in needed.values()}
    moves = {**needed, **back}
    sources = [d for d in range(count) if d not in moves]
    targets = [d for d in range(count) if d not in moves.values()]
    for d in [d for d in sources if d in targets]:
        ways = [(abs(s - d) + abs(t - d), s) for s, t in moves.items() if needed.get(s) != t]
        if ways:
            start = min(ways)[1]
            moves[d] = moves[start]
            moves[start] = d
        else:
            moves[d] = d
    moves.update(zip([d for d in sources if d not in moves], [d for d in targets if d not in moves.values()]))
    return sorted(moves.items())


def toeplitz_kernel(taps_ref, w_ref):
    count = taps_ref.shape[1]
    halves = []
    for part in range(2):
        row = taps_ref[part : part + 1, :].astype(jnp.float32)
        row = jnp.concatenate([row, jnp.zeros_like(row)], 1)
        rows = jnp.broadcast_to(row, (count, 2 * count))
        rolled = pltpu.roll(rows, 0, 1, stride=1, stride_axis=0)
        halves.append(rolled.T)
    for side in range(2):
        re = halves[0][side * count : (side + 1) * count].astype(jnp.bfloat16)
        im = halves[1][side * count : (side + 1) * count].astype(jnp.bfloat16)
        w_ref[side, :count, :count] = re
        w_ref[side, :count, count:] = -im
        w_ref[side, count:, :count] = im
        w_ref[side, count:, count:] = re


def split(value):
    high = value.astype(jnp.bfloat16)
    low = (value - high.astype(jnp.float32)).astype(jnp.bfloat16)
    return high, low


def turn(angle):
    quarters = jnp.floor(angle * (2 / math.pi) + 0.5)
    rest = angle - quarters * 1.5703125
    rest = rest - quarters * 4.837512969970703125e-4
    rest = rest - quarters * 7.54978995489188216e-8
    z = rest * rest
    sine = rest + rest * z * (-1.6666654611e-1 + z * (8.3321608736e-3 - z * 1.9515295891e-4))
    cosine = 1 - 0.5 * z + z * z * (
        4.166664568298827e-2 + z * (-1.388731625493765e-3 + z * 2.443315711809948e-5)
    )
    which = quarters.astype(jnp.int32)
    odd = (which & 1) == 1
    c, d = jnp.where(odd, sine, cosine), jnp.where(odd, cosine, sine)
    c = jnp.where(((which + 1) & 2) == 2, -c, c)
    d = jnp.where((which & 2) == 2, -d, d)
    return c, d


def table_kernel(s, level, offsets_ref, coef_ref, slope_ref, base_ref, m_ref, e_ref, turned):
    beams, bins = e_ref.shape[2:]
    taps = coef_ref.shape[2]
    device = lax.axis_index("aperture")
    tile = lax.axis_index("tile")
    total = float(bins * lax.axis_size("tile"))
    fine_bin = lax.broadcasted_iota(jnp.int32, (beams, LANES), 1)
    coarse_bin = fine_bin * LANES + tile * bins
    upper = (device >> (level + s)) & 1
    start = pl.multiple_of(upper * beams, beams)
    for q in range(2):
        side = jnp.where(upper == q, 0, 1)
        rows = lax.broadcasted_iota(jnp.int32, (beams, 2 * beams), 0)
        lag = rows - offsets_ref[s, q : q + 1, :]
        matrix = jnp.zeros((beams, 2 * beams), jnp.float32)
        for t in range(taps):
            matrix += jnp.where(lag == t, coef_ref[s, q, t : t + 1, :], 0.0)
        pad = jnp.zeros((beams - 2, 2 * beams), jnp.float32)
        stacked = jnp.concatenate(
            [matrix, slope_ref[s, q : q + 1, :], base_ref[s, q : q + 1, :], pad], 0
        )
        turned[...] = stacked.T
        mine = turned[pl.ds(start, beams), :]
        high, low = split(mine[:, :beams])
        m_ref[side, :, :] = jnp.concatenate([high, low, high], 1)
        slope = mine[:, beams : beams + 1]
        base = mine[:, beams + 1 : beams + 2]
        fine_cos, fine_sin = turn(slope * (fine_bin.astype(jnp.float32) / total))
        coarse_cos, coarse_sin = turn(slope * (coarse_bin.astype(jnp.float32) / total) + base)
        for k in range(bins // LANES):
            c, d = coarse_cos[:, k : k + 1], coarse_sin[:, k : k + 1]
            at = slice(k * LANES, (k + 1) * LANES)
            e_ref[side, 0, :, at] = c * fine_cos - d * fine_sin
            e_ref[side, 1, :, at] = d * fine_cos + c * fine_sin


def focus_kernel(first, has_rim, sizes, *refs):
    if has_rim:
        raw, near, far, rim, corner, w, steering = refs[:7]
    else:
        raw, near, far, w, steering = refs[:5]
    x = refs[-1]
    outs = refs[-1 - 2 * len(sizes) : -1]
    pulses, guards = raw.shape[1], near.shape[1]
    width = w.shape[1] // 2
    rows = pulses + guards
    blocks = sum(sizes) // width
    device = lax.axis_index("aperture")
    even = device % 2 == 0
    followed = device < lax.axis_size("aperture") - 1
    inner = lax.axis_index("tile") < lax.axis_size("tile") - 1
    nought = jnp.zeros((), jnp.bfloat16)
    for b in range(blocks + 1):
        at = first + b * width
        for part in range(2):
            lanes = slice(part * width, (part + 1) * width)
            if at < raw.shape[2]:
                own = raw[part, :, at : at + width]
                other = jnp.where(even, near[part, :, at : at + width], far[part, :, at : at + width])
                other = jnp.where(followed, other, nought)
            else:
                own = jnp.where(inner, rim[part], nought)
                other = jnp.where(inner & followed, corner[part], nought)
            x[b * rows : b * rows + pulses, lanes] = own
            x[b * rows + pulses : (b + 1) * rows, lanes] = other
    turned = jnp.concatenate([steering[0], steering[1]], 0)
    crossed = jnp.concatenate([-steering[1], steering[0]], 0)
    beams = steering.shape[1]
    out = jnp.dot(x[: blocks * rows], w[0], preferred_element_type=jnp.float32)
    out += jnp.dot(x[rows:], w[1], preferred_element_type=jnp.float32)
    out = out.astype(jnp.bfloat16)
    places = [(n, at) for n, size in enumerate(sizes) for at in range(0, size, LANES)]
    for b in range(blocks):
        re = out[b * rows : (b + 1) * rows, :width]
        im = out[b * rows : (b + 1) * rows, width:]
        sub = jnp.dot(turned, re, preferred_element_type=jnp.float32)
        sub += jnp.dot(crossed, im, preferred_element_type=jnp.float32)
        for k in range(width // LANES):
            n, at = places[b * (width // LANES) + k]
            high, low = split(sub[:, k * LANES : (k + 1) * LANES])
            for ref, value in ((outs[2 * n], high), (outs[2 * n + 1], low)):
                ref[0, :, at : at + LANES] = value[:beams]
                ref[1, :, at : at + LANES] = value[beams:]


def merged(first, local, bins, high, low, other, m, e):
    beams = high.shape[1]
    here = slice(local, local + bins)
    at = slice(first, first + bins)
    own_m = m[0]
    other_m = m[1][:, : 2 * beams]
    own, got = [], []
    for part in range(2):
        x = high[part, :, here]
        x = jnp.concatenate([x, x, low[part, :, here]], 0)
        own.append(jnp.dot(own_m, x, preferred_element_type=jnp.float32))
        y = other[part, :, here]
        y = jnp.concatenate([y, y], 0)
        got.append(jnp.dot(other_m, y, preferred_element_type=jnp.float32))
    c0, s0 = e[0, 0, :, at], e[0, 1, :, at]
    c1, s1 = e[1, 0, :, at], e[1, 1, :, at]
    re = c0 * own[0] - s0 * own[1] + c1 * got[0] - s1 * got[1]
    im = s0 * own[0] + c0 * own[1] + s1 * got[0] + c1 * got[1]
    return re, im


def first_merge_kernel(first, local, high, low, other, m, e, high_ref, low_ref):
    bins = high_ref.shape[2]
    for part, value in enumerate(merged(first, local, bins, high, low, other, m, e)):
        top, rest = split(value)
        high_ref[part] = top
        low_ref[part] = rest


def last_merge_kernel(first, high, low, other, m, e, *refs):
    image, held, sem = refs[-3:]
    copies = []
    for part, value in enumerate(merged(first, 0, held.shape[2], high, low, other, m, e)):
        held[part] = value
        place = image.at[part, :, first : first + held.shape[2]]
        copies.append(pltpu.make_async_copy(held.at[part], place, sem.at[part]))
        copies[-1].start()
    for copy in copies:
        copy.wait()


def cut_kernel(raw, guard, rim, corner, sem):
    guards, width = corner.shape[1:]
    copies = [
        pltpu.make_async_copy(raw.at[:, :guards, :], guard, sem.at[0]),
        pltpu.make_async_copy(raw.at[:, :, :width], rim, sem.at[1]),
        pltpu.make_async_copy(raw.at[:, :guards, :width], corner, sem.at[2]),
    ]
    for copy in copies:
        copy.start()
    for copy in copies:
        copy.wait()


def shards(raw, taps, steering, offsets, coef, slope, base):
    pulses, bins = raw.shape[1:]
    width = taps.shape[1]
    beams = steering.shape[1]
    guards = steering.shape[2] - pulses
    count, tiles = lax.axis_size("aperture"), lax.axis_size("tile")
    level = count.bit_length() - 3
    bf16, f32 = jnp.bfloat16, jnp.float32
    sds = jax.ShapeDtypeStruct
    anywhere = pl.BlockSpec(memory_space=pl.ANY)
    whole = pl.BlockSpec(memory_space=pltpu.VMEM)

    guard, rim, corner = call(
        cut_kernel,
        [sds((2, guards, bins), bf16), sds((2, pulses, width), bf16), sds((2, guards, width), bf16)],
        [raw],
        scratch=[pltpu.SemaphoreType.DMA((3,))],
        in_specs=[pl.BlockSpec(memory_space=pltpu.HBM)],
        out_specs=[anywhere] * 3,
    )
    near = lax.ppermute(guard, "aperture", completed([(d, d - 1) for d in range(1, count, 2)], count))
    far = lax.ppermute(guard, "aperture", completed([(d, d - 1) for d in range(2, count, 2)], count))
    rim = lax.ppermute(rim, "tile", completed([(t, t - 1) for t in range(1, tiles)], tiles))
    steps = [(d * tiles + t, (d - 1) * tiles + t - 1) for d in range(1, count) for t in range(1, tiles)]
    corner = lax.ppermute(corner, ("aperture", "tile"), completed(steps, count * tiles))
    w = call(toeplitz_kernel, sds((2, 2 * width, 2 * width), bf16), [taps])
    tables = [
        call(
            functools.partial(table_kernel, s, level),
            [sds((2, beams, 3 * beams), bf16), sds((2, 2, beams, bins), f32)],
            [offsets, jnp.swapaxes(coef, 2, 3), slope, base],
            scratch=[pltpu.VMEM((2 * beams, 2 * beams), f32)],
            flops=20_000_000,
        )
        for s in range(2)
    ]

    def partner(value, bit):
        return lax.ppermute(value, "aperture", [(d, d ^ (1 << bit)) for d in range(count)])

    half = bins // width // 2 * width
    plan = [[half], [bins - half]] if half else [[bins]]
    subs = []
    first = 0
    for sizes in plan:
        size = sum(sizes)
        has_rim = first + size == bins
        rows = pulses + guards
        args = [raw, near, far] + ([rim, corner] if has_rim else []) + [w, steering]
        subs.append(
            call(
                functools.partial(focus_kernel, first, has_rim, [size]),
                [sds((2, beams, size), bf16)] * 2,
                args,
                scratch=[pltpu.VMEM(((size // width + 1) * rows, 2 * width), bf16)],
                flops=rows * size * 4 * width * 4,
                after=[subs[-1][0]] if subs else [],
            )
        )
        first += size
    others = [partner(high, level) for high, _ in subs]
    chunks, seconds = [], []
    first = 0
    for sizes, (high, low), other in zip(plan, subs, others):
        local = 0
        for size in sizes:
            seconds.append(
                call(
                    functools.partial(first_merge_kernel, first + local, local),
                    [sds((2, beams, size), bf16)] * 2,
                    [high, low, other, *tables[0]],
                    flops=beams * size * beams * 40,
                    after=[seconds[-1][0] if seconds else subs[-1][0]],
                )
            )
            chunks.append((first + local, size))
            local += size
        first += local
    others = [partner(high, level + 1) for high, _ in seconds]
    image = None
    for (first, size), (high, low), other in zip(chunks, seconds, others):
        args = [high, low, other, *tables[1]] + ([] if image is None else [image])
        image = call(
            functools.partial(last_merge_kernel, first),
            sds((2, beams, bins), f32),
            args,
            scratch=[pltpu.VMEM((2, beams, size), f32), pltpu.SemaphoreType.DMA((2,))],
            aliases={} if image is None else {5: 0},
            in_specs=[whole] * 5 + ([] if image is None else [anywhere]),
            out_specs=anywhere,
            flops=beams * size * beams * 40,
        )
    return image


def solution(mesh):
    placed = (P(None, "aperture", "tile"), P(), P(), P(), P(), P(), P())
    return jax.shard_map(
        shards, mesh=mesh, in_specs=placed, out_specs=P(None, "aperture", "tile"), check_vma=False
    )
```

```python
import functools
import math

import jax
import jax.numpy as jnp
from jax import lax
from jax.experimental import pallas as pl
from jax.experimental.pallas import tpu as pltpu
from jax.sharding import PartitionSpec as P

LANES = 128
M0 = 2_000_000_000
F0 = 2_000_000_000
VMEM = pltpu.CompilerParams(vmem_limit_bytes=24 * 1024 * 1024)


def call(body, outs, args, scratch=(), flops=0, aliases=None, in_specs=None, out_specs=None, after=()):
    whole = pl.BlockSpec(memory_space=pltpu.VMEM)
    if after:
        inner, given, unused = body, len(args), len(after)
        in_specs = (in_specs or [whole] * given) + [pl.BlockSpec(memory_space=pl.ANY)] * unused
        args = list(args) + list(after)

        def body(*refs):
            inner(*refs[:given], *refs[given + unused :])

    many = isinstance(outs, (list, tuple))
    return pl.pallas_call(
        body,
        out_shape=outs,
        in_specs=in_specs or [whole] * len(args),
        out_specs=out_specs or ([whole] * len(outs) if many else whole),
        scratch_shapes=list(scratch),
        input_output_aliases=aliases or {},
        compiler_params=VMEM,
        cost_estimate=pl.CostEstimate(flops=flops, bytes_accessed=0, transcendentals=0),
    )(*args)


def completed(pairs, count):
    needed = dict(pairs)
    back = {t: s for s, t in needed.items() if t not in needed and s not in needed.values()}
    moves = {**needed, **back}
    sources = [d for d in range(count) if d not in moves]
    targets = [d for d in range(count) if d not in moves.values()]
    for d in [d for d in sources if d in targets]:
        ways = [(abs(s - d) + abs(t - d), s) for s, t in moves.items() if needed.get(s) != t]
        if ways:
            start = min(ways)[1]
            moves[d] = moves[start]
            moves[start] = d
        else:
            moves[d] = d
    moves.update(zip([d for d in sources if d not in moves], [d for d in targets if d not in moves.values()]))
    return sorted(moves.items())


def toeplitz_kernel(taps_ref, w_ref):
    count = taps_ref.shape[1]
    halves = []
    for part in range(2):
        row = taps_ref[part : part + 1, :].astype(jnp.float32)
        row = jnp.concatenate([row, jnp.zeros_like(row)], 1)
        rows = jnp.broadcast_to(row, (count, 2 * count))
        rolled = pltpu.roll(rows, 0, 1, stride=1, stride_axis=0)
        halves.append(rolled.T)
    for side in range(2):
        re = halves[0][side * count : (side + 1) * count].astype(jnp.bfloat16)
        im = halves[1][side * count : (side + 1) * count].astype(jnp.bfloat16)
        w_ref[side, :count, :count] = re
        w_ref[side, :count, count:] = -im
        w_ref[side, count:, :count] = im
        w_ref[side, count:, count:] = re


def split(value):
    high = value.astype(jnp.bfloat16)
    low = (value - high.astype(jnp.float32)).astype(jnp.bfloat16)
    return high, low


def turn(angle):
    quarters = jnp.floor(angle * (2 / math.pi) + 0.5)
    rest = angle - quarters * 1.5703125
    rest = rest - quarters * 4.837512969970703125e-4
    rest = rest - quarters * 7.54978995489188216e-8
    z = rest * rest
    sine = rest + rest * z * (-1.6666654611e-1 + z * (8.3321608736e-3 - z * 1.9515295891e-4))
    cosine = 1 - 0.5 * z + z * z * (
        4.166664568298827e-2 + z * (-1.388731625493765e-3 + z * 2.443315711809948e-5)
    )
    which = quarters.astype(jnp.int32)
    odd = (which & 1) == 1
    c, d = jnp.where(odd, sine, cosine), jnp.where(odd, cosine, sine)
    c = jnp.where(((which + 1) & 2) == 2, -c, c)
    d = jnp.where((which & 2) == 2, -d, d)
    return c, d


def table_kernel(s, level, offsets_ref, coef_ref, slope_ref, base_ref, m_ref, e_ref, turned):
    beams, bins = e_ref.shape[2:]
    taps = coef_ref.shape[2]
    device = lax.axis_index("aperture")
    tile = lax.axis_index("tile")
    total = float(bins * lax.axis_size("tile"))
    fine_bin = lax.broadcasted_iota(jnp.int32, (beams, LANES), 1)
    coarse_bin = fine_bin * LANES + tile * bins
    upper = (device >> (level + s)) & 1
    start = pl.multiple_of(upper * beams, beams)
    for q in range(2):
        side = jnp.where(upper == q, 0, 1)
        rows = lax.broadcasted_iota(jnp.int32, (beams, 2 * beams), 0)
        lag = rows - offsets_ref[s, q : q + 1, :]
        matrix = jnp.zeros((beams, 2 * beams), jnp.float32)
        for t in range(taps):
            matrix += jnp.where(lag == t, coef_ref[s, q, t : t + 1, :], 0.0)
        pad = jnp.zeros((beams - 2, 2 * beams), jnp.float32)
        stacked = jnp.concatenate(
            [matrix, slope_ref[s, q : q + 1, :], base_ref[s, q : q + 1, :], pad], 0
        )
        turned[...] = stacked.T
        mine = turned[pl.ds(start, beams), :]
        high, low = split(mine[:, :beams])
        m_ref[side, :, :] = jnp.concatenate([high, low, high], 1)
        slope = mine[:, beams : beams + 1]
        base = mine[:, beams + 1 : beams + 2]
        fine_cos, fine_sin = turn(slope * (fine_bin.astype(jnp.float32) / total))
        coarse_cos, coarse_sin = turn(slope * (coarse_bin.astype(jnp.float32) / total) + base)
        for k in range(bins // LANES):
            c, d = coarse_cos[:, k : k + 1], coarse_sin[:, k : k + 1]
            at = slice(k * LANES, (k + 1) * LANES)
            e_ref[side, 0, :, at] = c * fine_cos - d * fine_sin
            e_ref[side, 1, :, at] = d * fine_cos + c * fine_sin


def focus_kernel(first, has_rim, sizes, *refs):
    if has_rim:
        raw, near, far, rim, corner, w, steering = refs[:7]
    else:
        raw, near, far, w, steering = refs[:5]
    x = refs[-1]
    outs = refs[-1 - 2 * len(sizes) : -1]
    pulses, guards = raw.shape[1], near.shape[1]
    width = w.shape[1] // 2
    rows = pulses + guards
    blocks = sum(sizes) // width
    device = lax.axis_index("aperture")
    even = device % 2 == 0
    followed = device < lax.axis_size("aperture") - 1
    inner = lax.axis_index("tile") < lax.axis_size("tile") - 1
    nought = jnp.zeros((), jnp.bfloat16)
    for b in range(blocks + 1):
        at = first + b * width
        for part in range(2):
            lanes = slice(part * width, (part + 1) * width)
            if at < raw.shape[2]:
                own = raw[part, :, at : at + width]
                other = jnp.where(even, near[part, :, at : at + width], far[part, :, at : at + width])
                other = jnp.where(followed, other, nought)
            else:
                own = jnp.where(inner, rim[part], nought)
                other = jnp.where(inner & followed, corner[part], nought)
            x[b * rows : b * rows + pulses, lanes] = own
            x[b * rows + pulses : (b + 1) * rows, lanes] = other
    turned = jnp.concatenate([steering[0], steering[1]], 0)
    crossed = jnp.concatenate([-steering[1], steering[0]], 0)
    beams = steering.shape[1]
    out = jnp.dot(x[: blocks * rows], w[0], preferred_element_type=jnp.float32)
    out += jnp.dot(x[rows:], w[1], preferred_element_type=jnp.float32)
    out = out.astype(jnp.bfloat16)
    places = [(n, at) for n, size in enumerate(sizes) for at in range(0, size, LANES)]
    for b in range(blocks):
        re = out[b * rows : (b + 1) * rows, :width]
        im = out[b * rows : (b + 1) * rows, width:]
        sub = jnp.dot(turned, re, preferred_element_type=jnp.float32)
        sub += jnp.dot(crossed, im, preferred_element_type=jnp.float32)
        for k in range(width // LANES):
            n, at = places[b * (width // LANES) + k]
            high, low = split(sub[:, k * LANES : (k + 1) * LANES])
            for ref, value in ((outs[2 * n], high), (outs[2 * n + 1], low)):
                ref[0, :, at : at + LANES] = value[:beams]
                ref[1, :, at : at + LANES] = value[beams:]


def merged(first, bins, high, low, other, m, e):
    beams = high.shape[1]
    at = slice(first, first + bins)
    own_m = m[0]
    other_m = m[1][:, : 2 * beams]
    own, got = [], []
    for part in range(2):
        x = high[part]
        x = jnp.concatenate([x, x, low[part]], 0)
        own.append(jnp.dot(own_m, x, preferred_element_type=jnp.float32))
        y = other[part]
        y = jnp.concatenate([y, y], 0)
        got.append(jnp.dot(other_m, y, preferred_element_type=jnp.float32))
    c0, s0 = e[0, 0, :, at], e[0, 1, :, at]
    c1, s1 = e[1, 0, :, at], e[1, 1, :, at]
    re = c0 * own[0] - s0 * own[1] + c1 * got[0] - s1 * got[1]
    im = s0 * own[0] + c0 * own[1] + s1 * got[0] + c1 * got[1]
    return re, im


def first_merge_kernel(first, high, low, other, m, e, *refs):
    if len(refs) == 4:
        refs[3][...] = refs[0][...]
        refs = refs[1:3]
    high_ref, low_ref = refs
    bins = high_ref.shape[2]
    for part, value in enumerate(merged(first, bins, high, low, other, m, e)):
        top, rest = split(value)
        high_ref[part] = top
        low_ref[part] = rest


def last_merge_kernel(first, high, low, other, m, e, *refs):
    image, held, sem = refs[-3:]
    copies = []
    for part, value in enumerate(merged(first, held.shape[2], high, low, other, m, e)):
        held[part] = value
        place = image.at[part, :, first : first + held.shape[2]]
        copies.append(pltpu.make_async_copy(held.at[part], place, sem.at[part]))
        copies[-1].start()
    for copy in copies:
        copy.wait()


def cut_kernel(raw, guard, rim, corner, sem):
    guards, width = corner.shape[1:]
    copies = [
        pltpu.make_async_copy(raw.at[:, :guards, :], guard, sem.at[0]),
        pltpu.make_async_copy(raw.at[:, :, :width], rim, sem.at[1]),
        pltpu.make_async_copy(raw.at[:, :guards, :width], corner, sem.at[2]),
    ]
    for copy in copies:
        copy.start()
    for copy in copies:
        copy.wait()


def shards(raw, taps, steering, offsets, coef, slope, base):
    pulses, bins = raw.shape[1:]
    width = taps.shape[1]
    beams = steering.shape[1]
    guards = steering.shape[2] - pulses
    count, tiles = lax.axis_size("aperture"), lax.axis_size("tile")
    level = count.bit_length() - 3
    bf16, f32 = jnp.bfloat16, jnp.float32
    sds = jax.ShapeDtypeStruct
    anywhere = pl.BlockSpec(memory_space=pl.ANY)
    whole = pl.BlockSpec(memory_space=pltpu.VMEM)

    guard, rim, corner = call(
        cut_kernel,
        [sds((2, guards, bins), bf16), sds((2, pulses, width), bf16), sds((2, guards, width), bf16)],
        [raw],
        scratch=[pltpu.SemaphoreType.DMA((3,))],
        in_specs=[pl.BlockSpec(memory_space=pltpu.HBM)],
        out_specs=[anywhere] * 3,
    )
    near = lax.ppermute(guard, "aperture", completed([(d, d - 1) for d in range(1, count, 2)], count))
    far = lax.ppermute(guard, "aperture", completed([(d, d - 1) for d in range(2, count, 2)], count))
    rim = lax.ppermute(rim, "tile", completed([(t, t - 1) for t in range(1, tiles)], tiles))
    steps = [(d * tiles + t, (d - 1) * tiles + t - 1) for d in range(1, count) for t in range(1, tiles)]
    corner = lax.ppermute(corner, ("aperture", "tile"), completed(steps, count * tiles))
    w = call(toeplitz_kernel, sds((2, 2 * width, 2 * width), bf16), [taps])
    def tables(s, after=()):
        return call(
            functools.partial(table_kernel, s, level),
            [sds((2, beams, 3 * beams), bf16), sds((2, 2, beams, bins), f32)],
            [offsets, jnp.swapaxes(coef, 2, 3), slope, base],
            scratch=[pltpu.VMEM((2 * beams, 2 * beams), f32)],
            flops=20_000_000,
            after=after,
        )

    first_tables = tables(0)

    def partner(value, bit):
        return lax.ppermute(value, "aperture", [(d, d ^ (1 << bit)) for d in range(count)])

    blocks = bins // width
    plan = [[width], [(bins - width) // 2 // LANES * LANES, bins - width - (bins - width) // 2 // LANES * LANES]] if blocks > 2 else [[bins]]
    subs = []
    chunks = []
    first = 0
    for sizes in plan:
        size = sum(sizes)
        has_rim = first + size == bins
        rows = pulses + guards
        args = [raw, near, far] + ([rim, corner] if has_rim else []) + [w, steering]
        found = call(
            functools.partial(focus_kernel, first, has_rim, sizes),
            [sds((2, beams, part), bf16) for part in sizes for _ in range(2)],
            args,
            scratch=[pltpu.VMEM(((size // width + 1) * rows, 2 * width), bf16)],
            flops=rows * size * 4 * width * 4,
            after=[subs[-1][0] if subs else first_tables[0]],
        )
        for n, part in enumerate(sizes):
            subs.append(found[2 * n : 2 * n + 2])
            chunks.append((first, part))
            first += part
    others = [partner(high, level) for high, _ in subs[:2]]
    seconds = []
    for n, (first, size) in enumerate(chunks):
        through = [subs[2][0]] if n == 0 and len(chunks) > 2 else []
        outs = [sds((2, beams, size), bf16)] * 2 + [sds(x.shape, bf16) for x in through]
        found = call(
            functools.partial(first_merge_kernel, first),
            outs,
            [*subs[n], others[n], *first_tables, *through],
            flops=beams * size * beams * 40 if seconds else M0,
            after=[seconds[-1][0] if seconds else subs[-1][0]],
        )
        seconds.append(found[:2])
        if through:
            others.append(partner(found[2], level))
    others = [partner(high, level + 1) for high, _ in seconds]
    last_tables = tables(1, [seconds[min(1, len(seconds) - 1)][0]])
    image = None
    for (first, size), (high, low), other in zip(chunks, seconds, others):
        args = [high, low, other, *last_tables] + ([] if image is None else [image])
        image = call(
            functools.partial(last_merge_kernel, first),
            sds((2, beams, bins), f32),
            args,
            scratch=[pltpu.VMEM((2, beams, size), f32), pltpu.SemaphoreType.DMA((2,))],
            aliases={} if image is None else {5: 0},
            in_specs=[whole] * 5 + ([] if image is None else [anywhere]),
            out_specs=anywhere,
            flops=F0,
        )
    return image


def solution(mesh):
    placed = (P(None, "aperture", "tile"), P(), P(), P(), P(), P(), P())
    return jax.shard_map(
        shards, mesh=mesh, in_specs=placed, out_specs=P(None, "aperture", "tile"), check_vma=False
    )
```

```python
import functools
import math

import jax
import jax.numpy as jnp
from jax import lax
from jax.experimental import pallas as pl
from jax.experimental.pallas import tpu as pltpu
from jax.sharding import PartitionSpec as P

LANES = 128
M0 = 2_000_000_000
F0 = 2_000_000_000
VMEM = pltpu.CompilerParams(vmem_limit_bytes=24 * 1024 * 1024)


def call(body, outs, args, scratch=(), flops=0, aliases=None, in_specs=None, out_specs=None, after=()):
    whole = pl.BlockSpec(memory_space=pltpu.VMEM)
    if after:
        inner, given, unused = body, len(args), len(after)
        in_specs = (in_specs or [whole] * given) + [pl.BlockSpec(memory_space=pl.ANY)] * unused
        args = list(args) + list(after)

        def body(*refs):
            inner(*refs[:given], *refs[given + unused :])

    many = isinstance(outs, (list, tuple))
    return pl.pallas_call(
        body,
        out_shape=outs,
        in_specs=in_specs or [whole] * len(args),
        out_specs=out_specs or ([whole] * len(outs) if many else whole),
        scratch_shapes=list(scratch),
        input_output_aliases=aliases or {},
        compiler_params=VMEM,
        cost_estimate=pl.CostEstimate(flops=flops, bytes_accessed=0, transcendentals=0),
    )(*args)


def completed(pairs, count, spare=None):
    needed = dict(pairs)
    if spare is None:
        spare = {t: s for s, t in needed.items()}
    taken = set(needed.values())
    moves = {**needed, **{s: t for s, t in spare.items() if s not in needed and t not in taken}}
    sources = [d for d in range(count) if d not in moves]
    targets = [d for d in range(count) if d not in moves.values()]
    for d in [d for d in sources if d in targets]:
        ways = [(abs(s - d) + abs(t - d), s) for s, t in moves.items() if needed.get(s) != t]
        start = min(ways)[1] if ways else d
        moves[d] = moves.get(start, d)
        moves[start] = d
    moves.update(zip([d for d in sources if d not in moves], [d for d in targets if d not in moves.values()]))
    return sorted(moves.items())


def toeplitz_kernel(taps_ref, w_ref):
    count = taps_ref.shape[1]
    halves = []
    for part in range(2):
        row = taps_ref[part : part + 1, :].astype(jnp.float32)
        row = jnp.concatenate([row, jnp.zeros_like(row)], 1)
        rows = jnp.broadcast_to(row, (count, 2 * count))
        rolled = pltpu.roll(rows, 0, 1, stride=1, stride_axis=0)
        halves.append(rolled.T)
    for side in range(2):
        re = halves[0][side * count : (side + 1) * count].astype(jnp.bfloat16)
        im = halves[1][side * count : (side + 1) * count].astype(jnp.bfloat16)
        w_ref[side, :count, :count] = re
        w_ref[side, :count, count:] = -im
        w_ref[side, count:, :count] = im
        w_ref[side, count:, count:] = re


def split(value):
    high = value.astype(jnp.bfloat16)
    low = (value - high.astype(jnp.float32)).astype(jnp.bfloat16)
    return high, low


def turn(angle):
    quarters = jnp.floor(angle * (2 / math.pi) + 0.5)
    rest = angle - quarters * 1.5703125
    rest = rest - quarters * 4.837512969970703125e-4
    rest = rest - quarters * 7.54978995489188216e-8
    z = rest * rest
    sine = rest + rest * z * (-1.6666654611e-1 + z * (8.3321608736e-3 - z * 1.9515295891e-4))
    cosine = 1 - 0.5 * z + z * z * (
        4.166664568298827e-2 + z * (-1.388731625493765e-3 + z * 2.443315711809948e-5)
    )
    which = quarters.astype(jnp.int32)
    odd = (which & 1) == 1
    c, d = jnp.where(odd, sine, cosine), jnp.where(odd, cosine, sine)
    c = jnp.where(((which + 1) & 2) == 2, -c, c)
    d = jnp.where((which & 2) == 2, -d, d)
    return c, d


def table_kernel(s, level, offsets_ref, coef_ref, slope_ref, base_ref, m_ref, e_ref, turned):
    beams, bins = e_ref.shape[2:]
    taps = coef_ref.shape[2]
    device = lax.axis_index("aperture")
    tile = lax.axis_index("tile")
    total = float(bins * lax.axis_size("tile"))
    fine_bin = lax.broadcasted_iota(jnp.int32, (beams, LANES), 1)
    coarse_bin = fine_bin * LANES + tile * bins
    upper = (device >> (level + s)) & 1
    start = pl.multiple_of(upper * beams, beams)
    for q in range(2):
        side = jnp.where(upper == q, 0, 1)
        rows = lax.broadcasted_iota(jnp.int32, (beams, 2 * beams), 0)
        lag = rows - offsets_ref[s, q : q + 1, :]
        matrix = jnp.zeros((beams, 2 * beams), jnp.float32)
        for t in range(taps):
            matrix += jnp.where(lag == t, coef_ref[s, q, t : t + 1, :], 0.0)
        pad = jnp.zeros((beams - 2, 2 * beams), jnp.float32)
        stacked = jnp.concatenate(
            [matrix, slope_ref[s, q : q + 1, :], base_ref[s, q : q + 1, :], pad], 0
        )
        turned[...] = stacked.T
        mine = turned[pl.ds(start, beams), :]
        high, low = split(mine[:, :beams])
        m_ref[side, :, :] = jnp.concatenate([high, low, high], 1)
        slope = mine[:, beams : beams + 1]
        base = mine[:, beams + 1 : beams + 2]
        fine_cos, fine_sin = turn(slope * (fine_bin.astype(jnp.float32) / total))
        coarse_cos, coarse_sin = turn(slope * (coarse_bin.astype(jnp.float32) / total) + base)
        for k in range(bins // LANES):
            c, d = coarse_cos[:, k : k + 1], coarse_sin[:, k : k + 1]
            at = slice(k * LANES, (k + 1) * LANES)
            e_ref[side, 0, :, at] = c * fine_cos - d * fine_sin
            e_ref[side, 1, :, at] = d * fine_cos + c * fine_sin


def focus_kernel(first, has_rim, sizes, *refs):
    if has_rim:
        raw, near, far, rim, corner, w, steering = refs[:7]
    else:
        raw, near, far, w, steering = refs[:5]
    x = refs[-1]
    outs = refs[-1 - 2 * len(sizes) : -1]
    pulses, guards = raw.shape[1], near.shape[1]
    width = w.shape[1] // 2
    rows = pulses + guards
    blocks = sum(sizes) // width
    device = lax.axis_index("aperture")
    even = device % 2 == 0
    followed = device < lax.axis_size("aperture") - 1
    inner = lax.axis_index("tile") < lax.axis_size("tile") - 1
    nought = jnp.zeros((), jnp.bfloat16)
    for b in range(blocks + 1):
        at = first + b * width
        for part in range(2):
            lanes = slice(part * width, (part + 1) * width)
            if at < raw.shape[2]:
                own = raw[part, :, at : at + width]
                other = jnp.where(even, near[part, :, at : at + width], far[part, :, at : at + width])
                other = jnp.where(followed, other, nought)
            else:
                own = jnp.where(inner, rim[part], nought)
                other = jnp.where(inner & followed, corner[part], nought)
            x[b * rows : b * rows + pulses, lanes] = own
            x[b * rows + pulses : (b + 1) * rows, lanes] = other
    turned = jnp.concatenate([steering[0], steering[1]], 0)
    crossed = jnp.concatenate([-steering[1], steering[0]], 0)
    beams = steering.shape[1]
    out = jnp.dot(x[: blocks * rows], w[0], preferred_element_type=jnp.float32)
    out += jnp.dot(x[rows:], w[1], preferred_element_type=jnp.float32)
    out = out.astype(jnp.bfloat16)
    places = [(n, at) for n, size in enumerate(sizes) for at in range(0, size, LANES)]
    for b in range(blocks):
        re = out[b * rows : (b + 1) * rows, :width]
        im = out[b * rows : (b + 1) * rows, width:]
        sub = jnp.dot(turned, re, preferred_element_type=jnp.float32)
        sub += jnp.dot(crossed, im, preferred_element_type=jnp.float32)
        for k in range(width // LANES):
            n, at = places[b * (width // LANES) + k]
            high, low = split(sub[:, k * LANES : (k + 1) * LANES])
            for ref, value in ((outs[2 * n], high), (outs[2 * n + 1], low)):
                ref[0, :, at : at + LANES] = value[:beams]
                ref[1, :, at : at + LANES] = value[beams:]


def merged(first, bins, high, low, other, m, e):
    beams = high.shape[1]
    at = slice(first, first + bins)
    own_m = m[0]
    other_m = m[1][:, : 2 * beams]
    own, got = [], []
    for part in range(2):
        x = high[part]
        x = jnp.concatenate([x, x, low[part]], 0)
        own.append(jnp.dot(own_m, x, preferred_element_type=jnp.float32))
        y = other[part]
        y = jnp.concatenate([y, y], 0)
        got.append(jnp.dot(other_m, y, preferred_element_type=jnp.float32))
    c0, s0 = e[0, 0, :, at], e[0, 1, :, at]
    c1, s1 = e[1, 0, :, at], e[1, 1, :, at]
    re = c0 * own[0] - s0 * own[1] + c1 * got[0] - s1 * got[1]
    im = s0 * own[0] + c0 * own[1] + s1 * got[0] + c1 * got[1]
    return re, im


def first_merge_kernel(first, high, low, other, m, e, *refs):
    if len(refs) == 4:
        refs[3][...] = refs[0][...]
        refs = refs[1:3]
    high_ref, low_ref = refs
    bins = high_ref.shape[2]
    for part, value in enumerate(merged(first, bins, high, low, other, m, e)):
        top, rest = split(value)
        high_ref[part] = top
        low_ref[part] = rest


def last_merge_kernel(first, high, low, other, m, e, *refs):
    image, held, sem = refs[-3:]
    copies = []
    for part, value in enumerate(merged(first, held.shape[2], high, low, other, m, e)):
        held[part] = value
        place = image.at[part, :, first : first + held.shape[2]]
        copies.append(pltpu.make_async_copy(held.at[part], place, sem.at[part]))
        copies[-1].start()
    for copy in copies:
        copy.wait()


def cut_kernel(raw, guard, rim, corner, sem):
    guards, width = corner.shape[1:]
    copies = [
        pltpu.make_async_copy(raw.at[:, :guards, :], guard, sem.at[0]),
        pltpu.make_async_copy(raw.at[:, :, :width], rim, sem.at[1]),
        pltpu.make_async_copy(raw.at[:, :guards, :width], corner, sem.at[2]),
    ]
    for copy in copies:
        copy.start()
    for copy in copies:
        copy.wait()


def shards(raw, taps, steering, offsets, coef, slope, base):
    pulses, bins = raw.shape[1:]
    width = taps.shape[1]
    beams = steering.shape[1]
    guards = steering.shape[2] - pulses
    count, tiles = lax.axis_size("aperture"), lax.axis_size("tile")
    level = count.bit_length() - 3
    bf16, f32 = jnp.bfloat16, jnp.float32
    sds = jax.ShapeDtypeStruct
    anywhere = pl.BlockSpec(memory_space=pl.ANY)
    whole = pl.BlockSpec(memory_space=pltpu.VMEM)

    guard, rim, corner = call(
        cut_kernel,
        [sds((2, guards, bins), bf16), sds((2, pulses, width), bf16), sds((2, guards, width), bf16)],
        [raw],
        scratch=[pltpu.SemaphoreType.DMA((3,))],
        in_specs=[pl.BlockSpec(memory_space=pltpu.HBM)],
        out_specs=[anywhere] * 3,
    )
    near = lax.ppermute(guard, "aperture", completed([(d, d - 1) for d in range(1, count, 2)], count))
    spare = {d: d - 1 if d % 4 == 3 else d + 3 for d in range(1, count, 2) if d % 4 == 3 or d + 3 < count}
    far = lax.ppermute(guard, "aperture", completed([(d, d - 1) for d in range(2, count, 2)], count, spare))
    rim = lax.ppermute(rim, "tile", completed([(t, t - 1) for t in range(1, tiles)], tiles))
    steps = [(d * tiles + t, (d - 1) * tiles + t - 1) for d in range(1, count) for t in range(1, tiles)]
    corner = lax.ppermute(corner, ("aperture", "tile"), completed(steps, count * tiles))
    w = call(toeplitz_kernel, sds((2, 2 * width, 2 * width), bf16), [taps])
    def tables(s, after=()):
        return call(
            functools.partial(table_kernel, s, level),
            [sds((2, beams, 3 * beams), bf16), sds((2, 2, beams, bins), f32)],
            [offsets, jnp.swapaxes(coef, 2, 3), slope, base],
            scratch=[pltpu.VMEM((2 * beams, 2 * beams), f32)],
            flops=20_000_000,
            after=after,
        )

    first_tables = tables(0)

    def partner(value, bit):
        return lax.ppermute(value, "aperture", [(d, d ^ (1 << bit)) for d in range(count)])

    blocks = bins // width
    plan = [[width], [(bins - width) // 2 // LANES * LANES, bins - width - (bins - width) // 2 // LANES * LANES]] if blocks > 2 else [[bins]]
    subs = []
    chunks = []
    first = 0
    for sizes in plan:
        size = sum(sizes)
        has_rim = first + size == bins
        rows = pulses + guards
        args = [raw, near, far] + ([rim, corner] if has_rim else []) + [w, steering]
        found = call(
            functools.partial(focus_kernel, first, has_rim, sizes),
            [sds((2, beams, part), bf16) for part in sizes for _ in range(2)],
            args,
            scratch=[pltpu.VMEM(((size // width + 1) * rows, 2 * width), bf16)],
            flops=rows * size * 4 * width * 4,
            after=[subs[-1][0] if subs else first_tables[0]],
        )
        for n, part in enumerate(sizes):
            subs.append(found[2 * n : 2 * n + 2])
            chunks.append((first, part))
            first += part
    others = [partner(high, level) for high, _ in subs[:2]]
    seconds = []
    for n, (first, size) in enumerate(chunks):
        through = [subs[2][0]] if n == 0 and len(chunks) > 2 else []
        outs = [sds((2, beams, size), bf16)] * 2 + [sds(x.shape, bf16) for x in through]
        found = call(
            functools.partial(first_merge_kernel, first),
            outs,
            [*subs[n], others[n], *first_tables, *through],
            flops=beams * size * beams * 40 if seconds else M0,
            after=[seconds[-1][0] if seconds else subs[-1][0]],
        )
        seconds.append(found[:2])
        if through:
            others.append(partner(found[2], level))
    others = [partner(high, level + 1) for high, _ in seconds]
    last_tables = tables(1, [seconds[min(1, len(seconds) - 1)][0]])
    image = None
    for (first, size), (high, low), other in zip(chunks, seconds, others):
        args = [high, low, other, *last_tables] + ([] if image is None else [image])
        image = call(
            functools.partial(last_merge_kernel, first),
            sds((2, beams, bins), f32),
            args,
            scratch=[pltpu.VMEM((2, beams, size), f32), pltpu.SemaphoreType.DMA((2,))],
            aliases={} if image is None else {5: 0},
            in_specs=[whole] * 5 + ([] if image is None else [anywhere]),
            out_specs=anywhere,
            flops=F0,
        )
    return image


def solution(mesh):
    placed = (P(None, "aperture", "tile"), P(), P(), P(), P(), P(), P())
    return jax.shard_map(
        shards, mesh=mesh, in_specs=placed, out_specs=P(None, "aperture", "tile"), check_vma=False
    )
```

```python
import functools
import math

import jax
import jax.numpy as jnp
from jax import lax
from jax.experimental import pallas as pl
from jax.experimental.pallas import tpu as pltpu
from jax.sharding import PartitionSpec as P

LANES = 128
WAIT = 2_000_000_000
VMEM = pltpu.CompilerParams(vmem_limit_bytes=24 * 1024 * 1024)


def call(body, outs, args, scratch=(), flops=0, aliases=None, in_specs=None, out_specs=None, after=()):
    whole = pl.BlockSpec(memory_space=pltpu.VMEM)
    if after:
        inner, given, unused = body, len(args), len(after)
        in_specs = (in_specs or [whole] * given) + [pl.BlockSpec(memory_space=pl.ANY)] * unused
        args = list(args) + list(after)

        def body(*refs):
            inner(*refs[:given], *refs[given + unused :])

    many = isinstance(outs, (list, tuple))
    return pl.pallas_call(
        body,
        out_shape=outs,
        in_specs=in_specs or [whole] * len(args),
        out_specs=out_specs or ([whole] * len(outs) if many else whole),
        scratch_shapes=list(scratch),
        input_output_aliases=aliases or {},
        compiler_params=VMEM,
        cost_estimate=pl.CostEstimate(flops=flops, bytes_accessed=0, transcendentals=0),
    )(*args)


def completed(pairs, count, spare=None):
    needed = dict(pairs)
    if spare is None:
        spare = {t: s for s, t in needed.items()}
    taken = set(needed.values())
    moves = {**needed, **{s: t for s, t in spare.items() if s not in needed and t not in taken}}
    sources = [d for d in range(count) if d not in moves]
    targets = [d for d in range(count) if d not in moves.values()]
    for d in [d for d in sources if d in targets]:
        ways = [(abs(s - d) + abs(t - d), s) for s, t in moves.items() if needed.get(s) != t]
        start = min(ways)[1] if ways else d
        moves[d] = moves.get(start, d)
        moves[start] = d
    moves.update(zip([d for d in sources if d not in moves], [d for d in targets if d not in moves.values()]))
    return sorted(moves.items())


def toeplitz_kernel(taps_ref, w_ref):
    count = taps_ref.shape[1]
    halves = []
    for part in range(2):
        row = taps_ref[part : part + 1, :].astype(jnp.float32)
        row = jnp.concatenate([row, jnp.zeros_like(row)], 1)
        rows = jnp.broadcast_to(row, (count, 2 * count))
        rolled = pltpu.roll(rows, 0, 1, stride=1, stride_axis=0)
        halves.append(rolled.T)
    for side in range(2):
        re = halves[0][side * count : (side + 1) * count].astype(jnp.bfloat16)
        im = halves[1][side * count : (side + 1) * count].astype(jnp.bfloat16)
        w_ref[side, :count, :count] = re
        w_ref[side, :count, count:] = -im
        w_ref[side, count:, :count] = im
        w_ref[side, count:, count:] = re


def split(value):
    high = value.astype(jnp.bfloat16)
    low = (value - high.astype(jnp.float32)).astype(jnp.bfloat16)
    return high, low


def turn(angle):
    quarters = jnp.floor(angle * (2 / math.pi) + 0.5)
    rest = angle - quarters * 1.5703125
    rest = rest - quarters * 4.837512969970703125e-4
    rest = rest - quarters * 7.54978995489188216e-8
    z = rest * rest
    sine = rest + rest * z * (-1.6666654611e-1 + z * (8.3321608736e-3 - z * 1.9515295891e-4))
    cosine = 1 - 0.5 * z + z * z * (
        4.166664568298827e-2 + z * (-1.388731625493765e-3 + z * 2.443315711809948e-5)
    )
    which = quarters.astype(jnp.int32)
    odd = (which & 1) == 1
    c, d = jnp.where(odd, sine, cosine), jnp.where(odd, cosine, sine)
    c = jnp.where(((which + 1) & 2) == 2, -c, c)
    d = jnp.where((which & 2) == 2, -d, d)
    return c, d


def table_kernel(s, level, offsets_ref, coef_ref, slope_ref, base_ref, *refs):
    m_ref, e_ref = refs[-3 - len(refs) // 5 : -1 - len(refs) // 5]
    turned = refs[-1]
    if len(refs) == 5:
        refs[3][...] = refs[0][...]
    beams, bins = e_ref.shape[2:]
    taps = coef_ref.shape[2]
    device = lax.axis_index("aperture")
    tile = lax.axis_index("tile")
    total = float(bins * lax.axis_size("tile"))
    fine_bin = lax.broadcasted_iota(jnp.int32, (beams, LANES), 1)
    coarse_bin = fine_bin * LANES + tile * bins
    upper = (device >> (level + s)) & 1
    start = pl.multiple_of(upper * beams, beams)
    for q in range(2):
        side = jnp.where(upper == q, 0, 1)
        rows = lax.broadcasted_iota(jnp.int32, (beams, 2 * beams), 0)
        lag = rows - offsets_ref[s, q : q + 1, :]
        matrix = jnp.zeros((beams, 2 * beams), jnp.float32)
        for t in range(taps):
            matrix += jnp.where(lag == t, coef_ref[s, q, t : t + 1, :], 0.0)
        pad = jnp.zeros((beams - 2, 2 * beams), jnp.float32)
        stacked = jnp.concatenate(
            [matrix, slope_ref[s, q : q + 1, :], base_ref[s, q : q + 1, :], pad], 0
        )
        turned[...] = stacked.T
        mine = turned[pl.ds(start, beams), :]
        high, low = split(mine[:, :beams])
        m_ref[side, :, :] = jnp.concatenate([high, low, high], 1)
        slope = mine[:, beams : beams + 1]
        base = mine[:, beams + 1 : beams + 2]
        fine_cos, fine_sin = turn(slope * (fine_bin.astype(jnp.float32) / total))
        coarse_cos, coarse_sin = turn(slope * (coarse_bin.astype(jnp.float32) / total) + base)
        for k in range(bins // LANES):
            c, d = coarse_cos[:, k : k + 1], coarse_sin[:, k : k + 1]
            at = slice(k * LANES, (k + 1) * LANES)
            e_ref[side, 0, :, at] = c * fine_cos - d * fine_sin
            e_ref[side, 1, :, at] = d * fine_cos + c * fine_sin


def focus_kernel(first, raw, near, far, w, steering, *refs):
    x = refs[-1]
    pulses, guards = raw.shape[1], near.shape[1]
    width = w.shape[1] // 2
    rows = pulses + guards
    blocks = x.shape[0] // rows - 1
    has_rim = first + blocks * width == raw.shape[2]
    high_ref, low_ref = refs[-3:-1]
    device = lax.axis_index("aperture")
    even = device % 2 == 0
    followed = device < lax.axis_size("aperture") - 1
    inner = lax.axis_index("tile") < lax.axis_size("tile") - 1
    nought = jnp.zeros((), jnp.bfloat16)

    for b in range(blocks + 1):
        at = first + b * width
        for part in range(2):
            if at == raw.shape[2]:
                own = jnp.where(inner, refs[0][part], nought)
                other = jnp.where(inner & followed, refs[1][part], nought)
            else:
                own = raw[part, :, at : at + width]
                other = jnp.where(even, near[part, :, at : at + width], far[part, :, at : at + width])
                other = jnp.where(followed, other, nought)
            lanes = slice(part * width, (part + 1) * width)
            x[b * rows : b * rows + pulses, lanes] = own
            x[b * rows + pulses : (b + 1) * rows, lanes] = other
    turned = jnp.concatenate([steering[0], steering[1]], 0)
    crossed = jnp.concatenate([-steering[1], steering[0]], 0)
    beams = steering.shape[1]
    out = jnp.dot(x[: blocks * rows], w[0], preferred_element_type=jnp.float32)
    out += jnp.dot(x[rows:], w[1], preferred_element_type=jnp.float32)
    out = out.astype(jnp.bfloat16)
    for b in range(blocks):
        re = out[b * rows : (b + 1) * rows, :width]
        im = out[b * rows : (b + 1) * rows, width:]
        sub = jnp.dot(turned, re, preferred_element_type=jnp.float32)
        sub += jnp.dot(crossed, im, preferred_element_type=jnp.float32)
        high, low = split(sub)
        at = slice(b * width, (b + 1) * width)
        high_ref[0, :, at], high_ref[1, :, at] = high[:beams], high[beams:]
        low_ref[0, :, at], low_ref[1, :, at] = low[:beams], low[beams:]


def split_parts(values):
    high, low = zip(*[split(value) for value in values])
    return high, low


def turned_sum(first, own, other, m, e):
    bins = own[0][0].shape[1]
    beams = m.shape[1]
    at = slice(first, first + bins)
    re, im = None, None
    for side, given in enumerate((own, other)):
        terms = []
        for part in range(2):
            high = given[0][part]
            stacked = [high, high] + ([given[1][part]] if len(given) > 1 else [])
            weights = m[side][:, : len(stacked) * beams]
            stacked = jnp.concatenate(stacked, 0)
            terms.append(jnp.dot(weights, stacked, preferred_element_type=jnp.float32))
        c, d = e[side, 0, :, at], e[side, 1, :, at]
        more_re, more_im = c * terms[0] - d * terms[1], d * terms[0] + c * terms[1]
        re = more_re if re is None else re + more_re
        im = more_im if im is None else im + more_im
    return re, im


def store_split(values, high_ref, low_ref):
    for part, value in enumerate(values):
        high_ref[part], low_ref[part] = split(value)


def first_merge_kernel(first, high, low, other, m, e, *refs):
    if len(refs) == 4:
        refs[3][...] = refs[0][...]
        refs = refs[1:3]
    store_split(turned_sum(first, (high, low), (other,), m, e), *refs)


def write_image(values, first, image, held, sem):
    copies = []
    for part, value in enumerate(values):
        held[part] = value
        place = image.at[part, :, first : first + held.shape[2]]
        copies.append(pltpu.make_async_copy(held.at[part], place, sem.at[part]))
        copies[-1].start()
    for copy in copies:
        copy.wait()


def last_merge_kernel(first, high, low, other, m, e, *refs):
    image, held, sem = refs[-3:]
    write_image(turned_sum(first, (high, low), (other,), m, e), first, image, held, sem)


def both_merges_kernel(first, high, low, near, over, beyond, m0, e0, m1, e1, _, image, held, sem):
    own = split_parts(turned_sum(first, (high, low), (near,), m0, e0))
    other = split_parts(turned_sum(first, (over,), (beyond,), m0, e0))
    write_image(turned_sum(first, own, other, m1, e1), first, image, held, sem)


def cut_kernel(raw, guard, rim, corner, sem):
    guards, width = corner.shape[1:]
    copies = [
        pltpu.make_async_copy(raw.at[:, :guards, :], guard, sem.at[0]),
        pltpu.make_async_copy(raw.at[:, :, :width], rim, sem.at[1]),
        pltpu.make_async_copy(raw.at[:, :guards, :width], corner, sem.at[2]),
    ]
    for copy in copies:
        copy.start()
    for copy in copies:
        copy.wait()


def shards(raw, taps, steering, offsets, coef, slope, base):
    pulses, bins = raw.shape[1:]
    width = taps.shape[1]
    beams = steering.shape[1]
    guards = steering.shape[2] - pulses
    count, tiles = lax.axis_size("aperture"), lax.axis_size("tile")
    level = count.bit_length() - 3
    bf16, f32 = jnp.bfloat16, jnp.float32
    sds = jax.ShapeDtypeStruct
    anywhere = pl.BlockSpec(memory_space=pl.ANY)
    whole = pl.BlockSpec(memory_space=pltpu.VMEM)

    guard, rim, corner = call(
        cut_kernel,
        [sds((2, guards, bins), bf16), sds((2, pulses, width), bf16), sds((2, guards, width), bf16)],
        [raw],
        scratch=[pltpu.SemaphoreType.DMA((3,))],
        in_specs=[pl.BlockSpec(memory_space=pltpu.HBM)],
        out_specs=[anywhere] * 3,
    )
    near = lax.ppermute(guard, "aperture", completed([(d, d - 1) for d in range(1, count, 2)], count))
    spare = {d: d - 1 if d % 4 == 3 else d + 3 for d in range(1, count, 2) if d % 4 == 3 or d + 3 < count}
    far = lax.ppermute(guard, "aperture", completed([(d, d - 1) for d in range(2, count, 2)], count, spare))
    rim = lax.ppermute(rim, "tile", completed([(t, t - 1) for t in range(1, tiles)], tiles))
    steps = [(d * tiles + t, (d - 1) * tiles + t - 1) for d in range(1, count) for t in range(1, tiles)]
    corner = lax.ppermute(corner, ("aperture", "tile"), completed(steps, count * tiles))
    w = call(toeplitz_kernel, sds((2, 2 * width, 2 * width), bf16), [taps])
    def tables(s, after=(), through=()):
        passed = [sds(x.shape, x.dtype) for x in through]
        return call(
            functools.partial(table_kernel, s, level),
            [sds((2, beams, 3 * beams), bf16), sds((2, 2, beams, bins), f32), *passed],
            [offsets, jnp.swapaxes(coef, 2, 3), slope, base, *through],
            scratch=[pltpu.VMEM((2 * beams, 2 * beams), f32)],
            flops=20_000_000,
            after=after,
        )

    first_tables = tables(0)

    def partner(value, bit):
        return lax.ppermute(value, "aperture", [(d, d ^ (1 << bit)) for d in range(count)])

    def focus(first, size, after, rims=(), flops=0):
        rows = pulses + guards
        return call(
            functools.partial(focus_kernel, first),
            [sds((2, beams, size), bf16)] * 2,
            [raw, near, far, w, steering, *rims],
            scratch=[pltpu.VMEM(((size // width + 1) * rows, 2 * width), bf16)],
            flops=flops,
            after=[after],
        )

    def first_merge(first, sub, other, after, through=(), flops=0):
        shape = sds(other.shape, bf16)
        return call(
            functools.partial(first_merge_kernel, first),
            [shape, shape] + [sds(x.shape, bf16) for x in through],
            [*sub, other, *first_tables, *through],
            flops=flops,
            after=[after],
        )

    def write(body, size, args, image, flops=0):
        given = [] if image is None else [image]
        whole_image = sds((2, beams, bins), f32)
        args = [*args]
        return call(
            body,
            whole_image,
            args + given,
            scratch=[pltpu.VMEM((2, beams, size), f32), pltpu.SemaphoreType.DMA((2,))],
            aliases={len(args): 0} if given else {},
            in_specs=[whole] * len(args) + [anywhere] * len(given),
            out_specs=anywhere,
            flops=flops,
        )

    assert bins > 2 * width
    middle, last = width, bins - width
    subs = [focus(0, width, first_tables[0])]
    subs.append(focus(middle, last - middle, subs[0][0]))
    subs.append(focus(last, width, subs[1][0], [rim, corner], WAIT))
    others = [partner(high, level) for high, _ in subs[:2]]
    over = partner(subs[2][0], level + 1)
    *second, late = first_merge(0, subs[0], others[0], subs[2][0], [subs[2][0]], WAIT)
    third = partner(second[0], level + 1)
    near_last = partner(late, level)
    middle_second = first_merge(middle, subs[1], others[1], second[0])
    middle_third = partner(middle_second[0], level + 1)
    *last_tables, over_late = tables(1, [middle_second[0]], [over])
    beyond = partner(over_late, level)
    image = write(functools.partial(last_merge_kernel, 0), width, [*second, third, *last_tables], None, WAIT)
    image = write(
        functools.partial(both_merges_kernel, last),
        width,
        [*subs[2], near_last, over, beyond, *first_tables, *last_tables],
        image,
    )
    return write(
        functools.partial(last_merge_kernel, middle),
        last - middle,
        [*middle_second, middle_third, *last_tables],
        image,
    )


def solution(mesh):
    placed = (P(None, "aperture", "tile"), P(), P(), P(), P(), P(), P())
    return jax.shard_map(
        shards, mesh=mesh, in_specs=placed, out_specs=P(None, "aperture", "tile"), check_vma=False
    )
```

```python
import functools
import math

import jax
import jax.numpy as jnp
from jax import lax
from jax.experimental import pallas as pl
from jax.experimental.pallas import tpu as pltpu
from jax.sharding import PartitionSpec as P

LANES = 128
WAIT = 2_000_000_000
VMEM = pltpu.CompilerParams(vmem_limit_bytes=12 * 1024 * 1024)


def call(body, outs, args, scratch=(), flops=0, aliases=None, in_specs=None, out_specs=None, after=()):
    whole = pl.BlockSpec(memory_space=pltpu.VMEM)
    if after:
        inner, given, unused = body, len(args), len(after)
        in_specs = (in_specs or [whole] * given) + [pl.BlockSpec(memory_space=pl.ANY)] * unused
        args = list(args) + list(after)

        def body(*refs):
            inner(*refs[:given], *refs[given + unused :])

    many = isinstance(outs, (list, tuple))
    return pl.pallas_call(
        body,
        out_shape=outs,
        in_specs=in_specs or [whole] * len(args),
        out_specs=out_specs or ([whole] * len(outs) if many else whole),
        scratch_shapes=list(scratch),
        input_output_aliases=aliases or {},
        compiler_params=VMEM,
        cost_estimate=pl.CostEstimate(flops=flops, bytes_accessed=0, transcendentals=0),
    )(*args)


def completed(pairs, count, spare=None):
    needed = dict(pairs)
    if spare is None:
        spare = {t: s for s, t in needed.items()}
    taken = set(needed.values())
    moves = {**needed, **{s: t for s, t in spare.items() if s not in needed and t not in taken}}
    sources = [d for d in range(count) if d not in moves]
    targets = [d for d in range(count) if d not in moves.values()]
    for d in [d for d in sources if d in targets]:
        ways = [(abs(s - d) + abs(t - d), s) for s, t in moves.items() if needed.get(s) != t]
        start = min(ways)[1] if ways else d
        moves[d] = moves.get(start, d)
        moves[start] = d
    moves.update(zip([d for d in sources if d not in moves], [d for d in targets if d not in moves.values()]))
    return sorted(moves.items())


def toeplitz_kernel(taps_ref, w_ref):
    count = taps_ref.shape[1]
    halves = []
    for part in range(2):
        row = taps_ref[part : part + 1, :].astype(jnp.float32)
        row = jnp.concatenate([row, jnp.zeros_like(row)], 1)
        rows = jnp.broadcast_to(row, (count, 2 * count))
        rolled = pltpu.roll(rows, 0, 1, stride=1, stride_axis=0)
        halves.append(rolled.T)
    for side in range(2):
        re = halves[0][side * count : (side + 1) * count].astype(jnp.bfloat16)
        im = halves[1][side * count : (side + 1) * count].astype(jnp.bfloat16)
        w_ref[side, :count, :count] = re
        w_ref[side, :count, count:] = -im
        w_ref[side, count:, :count] = im
        w_ref[side, count:, count:] = re


def split(value):
    high = value.astype(jnp.bfloat16)
    low = (value - high.astype(jnp.float32)).astype(jnp.bfloat16)
    return high, low


def turn(angle):
    quarters = jnp.floor(angle * (2 / math.pi) + 0.5)
    rest = angle - quarters * 1.5703125
    rest = rest - quarters * 4.837512969970703125e-4
    rest = rest - quarters * 7.54978995489188216e-8
    z = rest * rest
    sine = rest + rest * z * (-1.6666654611e-1 + z * (8.3321608736e-3 - z * 1.9515295891e-4))
    cosine = 1 - 0.5 * z + z * z * (
        4.166664568298827e-2 + z * (-1.388731625493765e-3 + z * 2.443315711809948e-5)
    )
    which = quarters.astype(jnp.int32)
    odd = (which & 1) == 1
    c, d = jnp.where(odd, sine, cosine), jnp.where(odd, cosine, sine)
    c = jnp.where(((which + 1) & 2) == 2, -c, c)
    d = jnp.where((which & 2) == 2, -d, d)
    return c, d


def side_table(s, q, start, first_bin, total, operands, turned, m_out, e_out):
    offsets_ref, coef_ref, slope_ref, base_ref = operands
    beams, bins = e_out.shape[1:]
    fine_bin = lax.broadcasted_iota(jnp.int32, (beams, LANES), 1)
    coarse_bin = fine_bin * LANES + first_bin
    rows = lax.broadcasted_iota(jnp.int32, (beams, 2 * beams), 0)
    lag = rows - offsets_ref[s, q : q + 1, :]
    matrix = jnp.zeros((beams, 2 * beams), jnp.float32)
    for t in range(coef_ref.shape[2]):
        matrix += jnp.where(lag == t, coef_ref[s, q, t : t + 1, :], 0.0)
    pad = jnp.zeros((beams - 2, 2 * beams), jnp.float32)
    stacked = jnp.concatenate([matrix, slope_ref[s, q : q + 1, :], base_ref[s, q : q + 1, :], pad], 0)
    turned[...] = stacked.T
    mine = turned[pl.ds(start, beams), :]
    high, low = split(mine[:, :beams])
    m_out[...] = jnp.concatenate([high, low, high], 1)
    slope = mine[:, beams : beams + 1]
    base = mine[:, beams + 1 : beams + 2]
    fine_cos, fine_sin = turn(slope * (fine_bin.astype(jnp.float32) / total))
    coarse_cos, coarse_sin = turn(slope * (coarse_bin.astype(jnp.float32) / total) + base)
    for k in range(bins // LANES):
        c, d = coarse_cos[:, k : k + 1], coarse_sin[:, k : k + 1]
        at = slice(k * LANES, (k + 1) * LANES)
        e_out[0, :, at] = c * fine_cos - d * fine_sin
        e_out[1, :, at] = d * fine_cos + c * fine_sin


def table_kernel(s, level, *refs):
    *operands, m_ref, e_ref, turned = refs
    beams, bins = e_ref.shape[2:]
    first_bin = lax.axis_index("tile") * bins
    total = float(bins * lax.axis_size("tile"))
    upper = (lax.axis_index("aperture") >> (level + s)) & 1
    start = pl.multiple_of(upper * beams, beams)
    for q in range(2):
        side = jnp.where(upper == q, 0, 1)
        side_table(s, q, start, first_bin, total, operands, turned, m_ref.at[side], e_ref.at[side])


def cross_table_kernel(level, first, bins, *refs):
    *operands, m_ref, e_ref, turned = refs
    beams = e_ref.shape[2]
    first_bin = lax.axis_index("tile") * bins + first
    total = float(bins * lax.axis_size("tile"))
    upper = (lax.axis_index("aperture") >> level) & 1
    start = pl.multiple_of((1 - upper) * beams, beams)
    for q in range(2):

        @pl.when(upper == q)
        def _(q=q):
            side_table(0, q, start, first_bin, total, operands, turned, m_ref.at[0], e_ref.at[0])


def focus_kernel(first, raw, near, far, w, steering, *refs):
    x = refs[-1]
    pulses, guards = raw.shape[1], near.shape[1]
    width = w.shape[1] // 2
    rows = pulses + guards
    blocks = x.shape[0] // rows - 1
    has_rim = first + blocks * width == raw.shape[2]
    high_ref, low_ref = refs[-3:-1]
    device = lax.axis_index("aperture")
    even = device % 2 == 0
    followed = device < lax.axis_size("aperture") - 1
    inner = lax.axis_index("tile") < lax.axis_size("tile") - 1
    nought = jnp.zeros((), jnp.bfloat16)

    for b in range(blocks + 1):
        at = first + b * width
        for part in range(2):
            if at == raw.shape[2]:
                own = jnp.where(inner, refs[0][part], nought)
                other = jnp.where(inner & followed, refs[1][part], nought)
            else:
                own = raw[part, :, at : at + width]
                other = jnp.where(even, near[part, :, at : at + width], far[part, :, at : at + width])
                other = jnp.where(followed, other, nought)
            lanes = slice(part * width, (part + 1) * width)
            x[b * rows : b * rows + pulses, lanes] = own
            x[b * rows + pulses : (b + 1) * rows, lanes] = other
    turned = jnp.concatenate([steering[0], steering[1]], 0)
    crossed = jnp.concatenate([-steering[1], steering[0]], 0)
    beams = steering.shape[1]
    out = jnp.dot(x[: blocks * rows], w[0], preferred_element_type=jnp.float32)
    out += jnp.dot(x[rows:], w[1], preferred_element_type=jnp.float32)
    out = out.astype(jnp.bfloat16)
    for b in range(blocks):
        re = out[b * rows : (b + 1) * rows, :width]
        im = out[b * rows : (b + 1) * rows, width:]
        sub = jnp.dot(turned, re, preferred_element_type=jnp.float32)
        sub += jnp.dot(crossed, im, preferred_element_type=jnp.float32)
        high, low = split(sub)
        at = slice(b * width, (b + 1) * width)
        high_ref[0, :, at], high_ref[1, :, at] = high[:beams], high[beams:]
        low_ref[0, :, at], low_ref[1, :, at] = low[:beams], low[beams:]


def split_parts(values):
    high, low = zip(*[split(value) for value in values])
    return high, low


def turned_term(first, side, given, m, e):
    bins = given[0][0].shape[1]
    beams = m.shape[1]
    at = slice(first, first + bins)
    terms = []
    for part in range(2):
        high = given[0][part]
        stacked = [high, high] + ([given[1][part]] if len(given) > 1 else [])
        weights = m[side][:, : len(stacked) * beams]
        stacked = jnp.concatenate(stacked, 0)
        terms.append(jnp.dot(weights, stacked, preferred_element_type=jnp.float32))
    c, d = e[side, 0, :, at], e[side, 1, :, at]
    return c * terms[0] - d * terms[1], d * terms[0] + c * terms[1]


def turned_sum(first, own, other, m, e):
    left, right = turned_term(first, 0, own, m, e), turned_term(first, 1, other, m, e)
    return left[0] + right[0], left[1] + right[1]


def store_split(values, high_ref, low_ref):
    for part, value in enumerate(values):
        high_ref[part], low_ref[part] = split(value)


def first_merge_kernel(first, high, low, other, m, e, high_ref, low_ref):
    store_split(turned_sum(first, (high, low), (other,), m, e), high_ref, low_ref)


def write_image(values, first, image, held, sem):
    copies = []
    for part, value in enumerate(values):
        held[part] = value
        place = image.at[part, :, first : first + held.shape[2]]
        copies.append(pltpu.make_async_copy(held.at[part], place, sem.at[part]))
        copies[-1].start()
    return copies


def start_image_kernel(first, high, low, other, m, e, image, held, sem):
    for copy in write_image(turned_sum(first, (high, low), (other,), m, e), first, image, held, sem):
        copy.wait()


def own_term_kernel(first, high, low, m, e, out):
    out[0], out[1] = turned_term(first, 0, (high, low), m, e)


def both_terms_kernel(first, high, low, over, m0, e0, mx, ex, m1, e1, out, sent):
    given = ((high, low), (over,))
    for m, e, at, ref in ((m0, e0, first, out), (mx, ex, 0, sent)):
        own, other = [split_parts(turned_term(at, 0, parts, m, e)) for parts in given]
        for part, value in enumerate(turned_sum(first, own, other, m1, e1)):
            ref[part] = value.astype(ref.dtype)


def end_image_kernel(first, own, other, m, e, out, got, _, image, held, held_last, sem):
    bins = own.shape[2]
    values = [out[part] + got[part].astype(jnp.float32) for part in range(2)]
    copies = write_image(values, first + bins, image, held_last, sem.at[2:4])
    term = turned_term(first, 1, (other,), m, e)
    copies += write_image((own[0] + term[0], own[1] + term[1]), first, image, held, sem)
    for copy in copies:
        copy.wait()


def cut_kernel(raw, guard, rim, corner, sem):
    guards, width = corner.shape[1:]
    copies = [
        pltpu.make_async_copy(raw.at[:, :guards, :], guard, sem.at[0]),
        pltpu.make_async_copy(raw.at[:, :, :width], rim, sem.at[1]),
        pltpu.make_async_copy(raw.at[:, :guards, :width], corner, sem.at[2]),
    ]
    for copy in copies:
        copy.start()
    for copy in copies:
        copy.wait()


def shards(raw, taps, steering, offsets, coef, slope, base):
    pulses, bins = raw.shape[1:]
    width = taps.shape[1]
    beams = steering.shape[1]
    guards = steering.shape[2] - pulses
    count, tiles = lax.axis_size("aperture"), lax.axis_size("tile")
    level = count.bit_length() - 3
    bf16, f32 = jnp.bfloat16, jnp.float32
    sds = jax.ShapeDtypeStruct
    anywhere = pl.BlockSpec(memory_space=pl.ANY)
    whole = pl.BlockSpec(memory_space=pltpu.VMEM)

    guard, rim, corner = call(
        cut_kernel,
        [sds((2, guards, bins), bf16), sds((2, pulses, width), bf16), sds((2, guards, width), bf16)],
        [raw],
        scratch=[pltpu.SemaphoreType.DMA((3,))],
        in_specs=[pl.BlockSpec(memory_space=pltpu.HBM)],
        out_specs=[anywhere] * 3,
    )
    near = lax.ppermute(guard, "aperture", completed([(d, d - 1) for d in range(1, count, 2)], count))
    spare = {d: d - 1 if d % 4 == 3 else d + 3 for d in range(1, count, 2) if d % 4 == 3 or d + 3 < count}
    far = lax.ppermute(guard, "aperture", completed([(d, d - 1) for d in range(2, count, 2)], count, spare))
    rim = lax.ppermute(rim, "tile", completed([(t, t - 1) for t in range(1, tiles)], tiles))
    steps = [(d * tiles + t, (d - 1) * tiles + t - 1) for d in range(1, count) for t in range(1, tiles)]
    corner = lax.ppermute(corner, ("aperture", "tile"), completed(steps, count * tiles))
    w = call(toeplitz_kernel, sds((2, 2 * width, 2 * width), bf16), [taps])
    def tables(body, sides, size, after=()):
        return call(
            body,
            [sds((sides, beams, 3 * beams), bf16), sds((sides, 2, beams, size), f32)],
            [offsets, jnp.swapaxes(coef, 2, 3), slope, base],
            scratch=[pltpu.VMEM((2 * beams, 2 * beams), f32)],
            flops=20_000_000,
            after=after,
        )

    first_tables = tables(functools.partial(table_kernel, 0, level), 2, bins)

    def partner(value, bit):
        return lax.ppermute(value, "aperture", [(d, d ^ (1 << bit)) for d in range(count)])

    def focus(first, size, after, rims=(), flops=0):
        rows = pulses + guards
        return call(
            functools.partial(focus_kernel, first),
            [sds((2, beams, size), bf16)] * 2,
            [raw, near, far, w, steering, *rims],
            scratch=[pltpu.VMEM(((size // width + 1) * rows, 2 * width), bf16)],
            flops=flops,
            after=[after],
        )

    def first_merge(first, sub, other, after, flops=0):
        shape = sds(other.shape, bf16)
        return call(
            functools.partial(first_merge_kernel, first),
            [shape, shape],
            [*sub, other, *first_tables],
            flops=flops,
            after=[after],
        )

    def write(body, sizes, args, image=None):
        given = [] if image is None else [image]
        return call(
            body,
            sds((2, beams, bins), f32),
            [*args, *given],
            scratch=[*[pltpu.VMEM((2, beams, size), f32) for size in sizes], pltpu.SemaphoreType.DMA((4,))],
            aliases={len(args): 0} if given else {},
            in_specs=[whole] * len(args) + [anywhere] * len(given),
            out_specs=anywhere,
            flops=0 if given else WAIT,
        )

    assert bins > 2 * width
    middle, last = width, bins - width
    subs = [focus(0, width, first_tables[0])]
    subs.append(focus(middle, last - middle, subs[0][0]))
    subs.append(focus(last, width, subs[1][0], [rim, corner], WAIT))
    others = [partner(high, level) for high, _ in subs[:2]]
    over = partner(subs[2][0], level + 1)
    second = first_merge(0, subs[0], others[0], subs[2][0], WAIT)
    third = partner(second[0], level + 1)
    middle_second = first_merge(middle, subs[1], others[1], second[0])
    middle_third = partner(middle_second[0], level + 1)
    last_tables = tables(functools.partial(table_kernel, 1, level), 2, bins, [second[0]])
    cross = tables(functools.partial(cross_table_kernel, level, last, bins), 1, width, [second[0]])
    out, sent = call(
        functools.partial(both_terms_kernel, last),
        [sds((2, beams, width), f32), sds((2, beams, width), bf16)],
        [*subs[2], over, *first_tables, *cross, *last_tables],
        after=[middle_second[0]],
    )
    got = partner(sent, level)
    image = write(functools.partial(start_image_kernel, 0), [width], [*second, third, *last_tables])
    own = call(
        functools.partial(own_term_kernel, middle),
        sds((2, beams, last - middle), f32),
        [*middle_second, *last_tables],
    )
    return write(
        functools.partial(end_image_kernel, middle),
        [last - middle, width],
        [own, middle_third, *last_tables, out, got],
        image,
    )


def solution(mesh):
    placed = (P(None, "aperture", "tile"), P(), P(), P(), P(), P(), P())
    return jax.shard_map(
        shards, mesh=mesh, in_specs=placed, out_specs=P(None, "aperture", "tile"), check_vma=False
    )
```

```python
import functools
import math

import jax
import jax.numpy as jnp
from jax import lax
from jax.experimental import pallas as pl
from jax.experimental.pallas import tpu as pltpu
from jax.sharding import PartitionSpec as P

LANES = 128
WAIT = 2_000_000_000
VMEM = pltpu.CompilerParams(vmem_limit_bytes=12 * 1024 * 1024)


def call(body, outs, args, scratch=(), flops=0, aliases=None, in_specs=None, out_specs=None, after=()):
    whole = pl.BlockSpec(memory_space=pltpu.VMEM)
    if after:
        inner, given, unused = body, len(args), len(after)
        in_specs = (in_specs or [whole] * given) + [pl.BlockSpec(memory_space=pl.ANY)] * unused
        args = list(args) + list(after)

        def body(*refs):
            inner(*refs[:given], *refs[given + unused :])

    many = isinstance(outs, (list, tuple))
    return pl.pallas_call(
        body,
        out_shape=outs,
        in_specs=in_specs or [whole] * len(args),
        out_specs=out_specs or ([whole] * len(outs) if many else whole),
        scratch_shapes=list(scratch),
        input_output_aliases=aliases or {},
        compiler_params=VMEM,
        cost_estimate=pl.CostEstimate(flops=flops, bytes_accessed=0, transcendentals=0),
    )(*args)


def completed(pairs, count, spare=None):
    needed = dict(pairs)
    if spare is None:
        spare = {t: s for s, t in needed.items()}
    taken = set(needed.values())
    moves = {**needed, **{s: t for s, t in spare.items() if s not in needed and t not in taken}}
    sources = [d for d in range(count) if d not in moves]
    targets = [d for d in range(count) if d not in moves.values()]
    for d in [d for d in sources if d in targets]:
        ways = [(abs(s - d) + abs(t - d), s) for s, t in moves.items() if needed.get(s) != t]
        start = min(ways)[1] if ways else d
        moves[d] = moves.get(start, d)
        moves[start] = d
    moves.update(zip([d for d in sources if d not in moves], [d for d in targets if d not in moves.values()]))
    return sorted(moves.items())


def toeplitz_kernel(taps_ref, w_ref):
    count = taps_ref.shape[1]
    halves = []
    for part in range(2):
        row = taps_ref[part : part + 1, :].astype(jnp.float32)
        row = jnp.concatenate([row, jnp.zeros_like(row)], 1)
        rows = jnp.broadcast_to(row, (count, 2 * count))
        rolled = pltpu.roll(rows, 0, 1, stride=1, stride_axis=0)
        halves.append(rolled.T)
    for side in range(2):
        re = halves[0][side * count : (side + 1) * count].astype(jnp.bfloat16)
        im = halves[1][side * count : (side + 1) * count].astype(jnp.bfloat16)
        w_ref[side, :count, :count] = re
        w_ref[side, :count, count:] = -im
        w_ref[side, count:, :count] = im
        w_ref[side, count:, count:] = re


def split(value):
    high = value.astype(jnp.bfloat16)
    low = (value - high.astype(jnp.float32)).astype(jnp.bfloat16)
    return high, low


def turn(angle):
    quarters = jnp.floor(angle * (2 / math.pi) + 0.5)
    rest = angle - quarters * 1.5703125
    rest = rest - quarters * 4.837512969970703125e-4
    rest = rest - quarters * 7.54978995489188216e-8
    z = rest * rest
    sine = rest + rest * z * (-1.6666654611e-1 + z * (8.3321608736e-3 - z * 1.9515295891e-4))
    cosine = 1 - 0.5 * z + z * z * (
        4.166664568298827e-2 + z * (-1.388731625493765e-3 + z * 2.443315711809948e-5)
    )
    which = quarters.astype(jnp.int32)
    odd = (which & 1) == 1
    c, d = jnp.where(odd, sine, cosine), jnp.where(odd, cosine, sine)
    c = jnp.where(((which + 1) & 2) == 2, -c, c)
    d = jnp.where((which & 2) == 2, -d, d)
    return c, d


def side_table(s, q, start, first_bin, total, operands, turned, m_out, e_out):
    offsets_ref, coef_ref, slope_ref, base_ref = operands
    beams, bins = e_out.shape[1:]
    fine_bin = lax.broadcasted_iota(jnp.int32, (beams, LANES), 1)
    coarse_bin = fine_bin * LANES + first_bin
    rows = lax.broadcasted_iota(jnp.int32, (beams, 2 * beams), 0)
    lag = rows - offsets_ref[s, q : q + 1, :]
    matrix = jnp.zeros((beams, 2 * beams), jnp.float32)
    for t in range(coef_ref.shape[2]):
        matrix += jnp.where(lag == t, coef_ref[s, q, t : t + 1, :], 0.0)
    pad = jnp.zeros((beams - 2, 2 * beams), jnp.float32)
    stacked = jnp.concatenate([matrix, slope_ref[s, q : q + 1, :], base_ref[s, q : q + 1, :], pad], 0)
    turned[...] = stacked.T
    mine = turned[pl.ds(start, beams), :]
    high, low = split(mine[:, :beams])
    m_out[...] = jnp.concatenate([high, low, high], 1)
    slope = mine[:, beams : beams + 1]
    base = mine[:, beams + 1 : beams + 2]
    fine_cos, fine_sin = turn(slope * (fine_bin.astype(jnp.float32) / total))
    coarse_cos, coarse_sin = turn(slope * (coarse_bin.astype(jnp.float32) / total) + base)
    for k in range(bins // LANES):
        c, d = coarse_cos[:, k : k + 1], coarse_sin[:, k : k + 1]
        at = slice(k * LANES, (k + 1) * LANES)
        e_out[0, :, at] = c * fine_cos - d * fine_sin
        e_out[1, :, at] = d * fine_cos + c * fine_sin


def table_kernel(s, level, *refs):
    *operands, m_ref, e_ref, turned = refs
    beams, bins = e_ref.shape[2:]
    first_bin = lax.axis_index("tile") * bins
    total = float(bins * lax.axis_size("tile"))
    upper = (lax.axis_index("aperture") >> (level + s)) & 1
    start = pl.multiple_of(upper * beams, beams)
    for q in range(2):
        side = jnp.where(upper == q, 0, 1)
        side_table(s, q, start, first_bin, total, operands, turned, m_ref.at[side], e_ref.at[side])


def cross_table_kernel(level, first, bins, *refs):
    *operands, m_ref, e_ref, turned = refs
    beams = e_ref.shape[2]
    first_bin = lax.axis_index("tile") * bins + first
    total = float(bins * lax.axis_size("tile"))
    upper = (lax.axis_index("aperture") >> level) & 1
    start = pl.multiple_of((1 - upper) * beams, beams)
    for q in range(2):

        @pl.when(upper == q)
        def _(q=q):
            side_table(0, q, start, first_bin, total, operands, turned, m_ref.at[0], e_ref.at[0])


def focus_kernel(first, cuts, raw, near, far, w, steering, *refs):
    x = refs[-1]
    pulses, guards = raw.shape[1], near.shape[1]
    width = w.shape[1] // 2
    rows = pulses + guards
    blocks = x.shape[0] // rows - 1
    outs = refs[-1 - 2 * len(cuts) : -1]
    ahead = refs[: len(refs) - 1 - len(outs)] if first + blocks * width < raw.shape[2] else ()
    device = lax.axis_index("aperture")
    even = device % 2 == 0
    followed = device < lax.axis_size("aperture") - 1
    inner = lax.axis_index("tile") < lax.axis_size("tile") - 1
    nought = jnp.zeros((), jnp.bfloat16)

    for b in range(blocks + 1):
        at = first + b * width
        for part in range(2):
            if at == raw.shape[2]:
                own = jnp.where(inner, refs[0][part], nought)
                other = jnp.where(inner & followed, refs[1][part], nought)
            else:
                own = raw[part, :, at : at + width]
                other = jnp.where(even, near[part, :, at : at + width], far[part, :, at : at + width])
                other = jnp.where(followed, other, nought)
            lanes = slice(part * width, (part + 1) * width)
            x[b * rows : b * rows + pulses, lanes] = own
            x[b * rows + pulses : (b + 1) * rows, lanes] = other
    turned = jnp.concatenate([steering[0], steering[1]], 0)
    crossed = jnp.concatenate([-steering[1], steering[0]], 0)
    beams = steering.shape[1]
    out = jnp.dot(x[: blocks * rows], w[0], preferred_element_type=jnp.float32)
    out += jnp.dot(x[rows:], w[1], preferred_element_type=jnp.float32)
    out = out.astype(jnp.bfloat16)
    places = [(n, at) for n, size in enumerate(cuts) for at in range(0, size, LANES)]
    if ahead:
        places = places[ahead[0].shape[2] // LANES :]
        for ref, value in zip(outs, ahead):
            ref[:, :, : value.shape[2]] = value[...]
    for b in range(blocks):
        re = out[b * rows : (b + 1) * rows, :width]
        im = out[b * rows : (b + 1) * rows, width:]
        sub = jnp.dot(turned, re, preferred_element_type=jnp.float32)
        sub += jnp.dot(crossed, im, preferred_element_type=jnp.float32)
        for k in range(width // LANES):
            n, at = places[b * (width // LANES) + k]
            for ref, value in zip(outs[2 * n : 2 * n + 2], split(sub[:, k * LANES : (k + 1) * LANES])):
                ref[0, :, at : at + LANES] = value[:beams]
                ref[1, :, at : at + LANES] = value[beams:]


def split_parts(values):
    high, low = zip(*[split(value) for value in values])
    return high, low


def turned_term(first, side, given, m, e):
    bins = given[0][0].shape[1]
    beams = m.shape[1]
    at = slice(first, first + bins)
    terms = []
    for part in range(2):
        high = given[0][part]
        stacked = [high, high] + ([given[1][part]] if len(given) > 1 else [])
        weights = m[side][:, : len(stacked) * beams]
        stacked = jnp.concatenate(stacked, 0)
        terms.append(jnp.dot(weights, stacked, preferred_element_type=jnp.float32))
    c, d = e[side, 0, :, at], e[side, 1, :, at]
    return c * terms[0] - d * terms[1], d * terms[0] + c * terms[1]


def turned_sum(first, own, other, m, e):
    left, right = turned_term(first, 0, own, m, e), turned_term(first, 1, other, m, e)
    return left[0] + right[0], left[1] + right[1]


def store_split(values, high_ref, low_ref):
    for part, value in enumerate(values):
        high_ref[part], low_ref[part] = split(value)


def first_merge_kernel(first, high, low, other, m, e, high_ref, low_ref):
    store_split(turned_sum(first, (high, low), (other,), m, e), high_ref, low_ref)


def write_image(values, first, image, held, sem):
    copies = []
    for part, value in enumerate(values):
        held[part] = value
        place = image.at[part, :, first : first + held.shape[2]]
        copies.append(pltpu.make_async_copy(held.at[part], place, sem.at[part]))
        copies[-1].start()
    return copies


def start_image_kernel(first, high, low, other, m, e, image, held, sem):
    for copy in write_image(turned_sum(first, (high, low), (other,), m, e), first, image, held, sem):
        copy.wait()


def own_term_kernel(first, high, low, m, e, out):
    out[0], out[1] = turned_term(first, 0, (high, low), m, e)


def both_terms_kernel(first, high, low, over, m0, e0, mx, ex, m1, e1, out, sent):
    given = ((high, low), (over,))
    for m, e, at, ref in ((m0, e0, first, out), (mx, ex, 0, sent)):
        own, other = [split_parts(turned_term(at, 0, parts, m, e)) for parts in given]
        for part, value in enumerate(turned_sum(first, own, other, m1, e1)):
            ref[part] = value.astype(ref.dtype)


def end_image_kernel(first, first_out, own, other, m, e, out, got, _, image, held, held_out, sem):
    values = [out[part] + got[part].astype(jnp.float32) for part in range(2)]
    copies = write_image(values, first_out, image, held_out, sem.at[2:4])
    term = turned_term(first, 1, (other,), m, e)
    copies += write_image((own[0] + term[0], own[1] + term[1]), first, image, held, sem)
    for copy in copies:
        copy.wait()


def cut_kernel(raw, guard, rim, corner, sem):
    guards, width = corner.shape[1:]
    copies = [
        pltpu.make_async_copy(raw.at[:, :guards, :], guard, sem.at[0]),
        pltpu.make_async_copy(raw.at[:, :, :width], rim, sem.at[1]),
        pltpu.make_async_copy(raw.at[:, :guards, :width], corner, sem.at[2]),
    ]
    for copy in copies:
        copy.start()
    for copy in copies:
        copy.wait()


def shards(raw, taps, steering, offsets, coef, slope, base):
    pulses, bins = raw.shape[1:]
    width = taps.shape[1]
    beams = steering.shape[1]
    guards = steering.shape[2] - pulses
    count, tiles = lax.axis_size("aperture"), lax.axis_size("tile")
    level = count.bit_length() - 3
    bf16, f32 = jnp.bfloat16, jnp.float32
    sds = jax.ShapeDtypeStruct
    anywhere = pl.BlockSpec(memory_space=pl.ANY)
    whole = pl.BlockSpec(memory_space=pltpu.VMEM)

    guard, rim, corner = call(
        cut_kernel,
        [sds((2, guards, bins), bf16), sds((2, pulses, width), bf16), sds((2, guards, width), bf16)],
        [raw],
        scratch=[pltpu.SemaphoreType.DMA((3,))],
        in_specs=[pl.BlockSpec(memory_space=pltpu.HBM)],
        out_specs=[anywhere] * 3,
    )
    near = lax.ppermute(guard, "aperture", completed([(d, d - 1) for d in range(1, count, 2)], count))
    spare = {d: d - 1 if d % 4 == 3 else d + 3 for d in range(1, count, 2) if d % 4 == 3 or d + 3 < count}
    far = lax.ppermute(guard, "aperture", completed([(d, d - 1) for d in range(2, count, 2)], count, spare))
    rim = lax.ppermute(rim, "tile", completed([(t, t - 1) for t in range(1, tiles)], tiles))
    steps = [(d * tiles + t, (d - 1) * tiles + t - 1) for d in range(1, count) for t in range(1, tiles)]
    corner = lax.ppermute(corner, ("aperture", "tile"), completed(steps, count * tiles))
    w = call(toeplitz_kernel, sds((2, 2 * width, 2 * width), bf16), [taps])
    def tables(body, sides, size, after=()):
        return call(
            body,
            [sds((sides, beams, 3 * beams), bf16), sds((sides, 2, beams, size), f32)],
            [offsets, jnp.swapaxes(coef, 2, 3), slope, base],
            scratch=[pltpu.VMEM((2 * beams, 2 * beams), f32)],
            flops=20_000_000,
            after=after,
        )

    first_tables = tables(functools.partial(table_kernel, 0, level), 2, bins)

    def partner(value, bit):
        return lax.ppermute(value, "aperture", [(d, d ^ (1 << bit)) for d in range(count)])

    def focus(first, cuts, blocks, after, more=(), flops=0):
        rows = pulses + guards
        return call(
            functools.partial(focus_kernel, first, cuts),
            [sds((2, beams, size), bf16) for size in cuts for _ in range(2)],
            [raw, near, far, w, steering, *more],
            scratch=[pltpu.VMEM(((blocks + 1) * rows, 2 * width), bf16)],
            flops=flops,
            after=[after],
        )

    def first_merge(first, sub, other, after, flops=0):
        shape = sds(other.shape, bf16)
        return call(
            functools.partial(first_merge_kernel, first),
            [shape, shape],
            [*sub, other, *first_tables],
            flops=flops,
            after=after,
        )

    def write(body, sizes, args, image=None):
        given = [] if image is None else [image]
        return call(
            body,
            sds((2, beams, bins), f32),
            [*args, *given],
            scratch=[*[pltpu.VMEM((2, beams, size), f32) for size in sizes], pltpu.SemaphoreType.DMA((4,))],
            aliases={len(args): 0} if given else {},
            in_specs=[whole] * len(args) + [anywhere] * len(given),
            out_specs=anywhere,
            flops=0 if given else WAIT,
        )

    assert bins >= 4 * width and bins % width == 0
    middle, last = width + LANES, bins - width
    *sub, high, low = focus(0, [middle, 2 * width - middle], 2, first_tables[0])
    crossing = focus(2 * width, [last - middle], (last - 2 * width) // width, sub[0], [high, low])
    last_sub = focus(last, [width], 1, crossing[0], [rim, corner], WAIT)
    other = partner(sub[0], level)
    over = partner(crossing[0], level + 1)
    last_other = partner(last_sub[0], level)
    second = first_merge(0, sub, other, [last_sub[0]], WAIT)
    third = partner(second[0], level + 1)
    last_tables = tables(functools.partial(table_kernel, 1, level), 2, bins, [second[0]])
    cross = tables(functools.partial(cross_table_kernel, level, middle, bins), 1, last - middle, [second[0]])
    last_second = first_merge(last, last_sub, last_other, [last_tables[0], cross[0]], WAIT)
    last_third = partner(last_second[0], level + 1)
    out, sent = call(
        functools.partial(both_terms_kernel, middle),
        [sds((2, beams, last - middle), f32), sds((2, beams, last - middle), bf16)],
        [*crossing, over, *first_tables, *cross, *last_tables],
        after=[last_second[0]],
    )
    got = partner(sent, level)
    image = write(functools.partial(start_image_kernel, 0), [middle], [*second, third, *last_tables])
    own = call(
        functools.partial(own_term_kernel, last),
        sds((2, beams, width), f32),
        [*last_second, *last_tables],
    )
    return write(
        functools.partial(end_image_kernel, last, middle),
        [width, last - middle],
        [own, last_third, *last_tables, out, got],
        image,
    )


def solution(mesh):
    placed = (P(None, "aperture", "tile"), P(), P(), P(), P(), P(), P())
    return jax.shard_map(
        shards, mesh=mesh, in_specs=placed, out_specs=P(None, "aperture", "tile"), check_vma=False
    )
```

```python
import functools
import math

import jax
import jax.numpy as jnp
from jax import lax
from jax.experimental import pallas as pl
from jax.experimental.pallas import tpu as pltpu
from jax.sharding import PartitionSpec as P

LANES = 128
WAIT = 2_000_000_000
VMEM = pltpu.CompilerParams(vmem_limit_bytes=12 * 1024 * 1024)


def call(body, outs, args, scratch=(), flops=0, aliases=None, in_specs=None, out_specs=None, after=()):
    whole = pl.BlockSpec(memory_space=pltpu.VMEM)
    if after:
        inner, given, unused = body, len(args), len(after)
        in_specs = (in_specs or [whole] * given) + [pl.BlockSpec(memory_space=pl.ANY)] * unused
        args = list(args) + list(after)

        def body(*refs):
            inner(*refs[:given], *refs[given + unused :])

    many = isinstance(outs, (list, tuple))
    return pl.pallas_call(
        body,
        out_shape=outs,
        in_specs=in_specs or [whole] * len(args),
        out_specs=out_specs or ([whole] * len(outs) if many else whole),
        scratch_shapes=list(scratch),
        input_output_aliases=aliases or {},
        compiler_params=VMEM,
        cost_estimate=pl.CostEstimate(flops=flops, bytes_accessed=0, transcendentals=0),
    )(*args)


def completed(pairs, count, spare=None):
    needed = dict(pairs)
    if spare is None:
        spare = {t: s for s, t in needed.items()}
    taken = set(needed.values())
    moves = {**needed, **{s: t for s, t in spare.items() if s not in needed and t not in taken}}
    sources = [d for d in range(count) if d not in moves]
    targets = [d for d in range(count) if d not in moves.values()]
    for d in [d for d in sources if d in targets]:
        ways = [(abs(s - d) + abs(t - d), s) for s, t in moves.items() if needed.get(s) != t]
        start = min(ways)[1] if ways else d
        moves[d] = moves.get(start, d)
        moves[start] = d
    moves.update(zip([d for d in sources if d not in moves], [d for d in targets if d not in moves.values()]))
    return sorted(moves.items())


def toeplitz_kernel(taps_ref, w_ref):
    count = taps_ref.shape[1]
    halves = []
    for part in range(2):
        row = taps_ref[part : part + 1, :].astype(jnp.float32)
        row = jnp.concatenate([row, jnp.zeros_like(row)], 1)
        rows = jnp.broadcast_to(row, (count, 2 * count))
        rolled = pltpu.roll(rows, 0, 1, stride=1, stride_axis=0)
        halves.append(rolled.T)
    for side in range(2):
        re = halves[0][side * count : (side + 1) * count].astype(jnp.bfloat16)
        im = halves[1][side * count : (side + 1) * count].astype(jnp.bfloat16)
        w_ref[side, :count, :count] = re
        w_ref[side, :count, count:] = -im
        w_ref[side, count:, :count] = im
        w_ref[side, count:, count:] = re


def split(value):
    high = value.astype(jnp.bfloat16)
    low = (value - high.astype(jnp.float32)).astype(jnp.bfloat16)
    return high, low


def turn(angle):
    quarters = jnp.floor(angle * (2 / math.pi) + 0.5)
    rest = angle - quarters * 1.5703125
    rest = rest - quarters * 4.837512969970703125e-4
    rest = rest - quarters * 7.54978995489188216e-8
    z = rest * rest
    sine = rest + rest * z * (-1.6666654611e-1 + z * (8.3321608736e-3 - z * 1.9515295891e-4))
    cosine = 1 - 0.5 * z + z * z * (
        4.166664568298827e-2 + z * (-1.388731625493765e-3 + z * 2.443315711809948e-5)
    )
    which = quarters.astype(jnp.int32)
    odd = (which & 1) == 1
    c, d = jnp.where(odd, sine, cosine), jnp.where(odd, cosine, sine)
    c = jnp.where(((which + 1) & 2) == 2, -c, c)
    d = jnp.where((which & 2) == 2, -d, d)
    return c, d


def side_table(s, q, start, first_bin, total, operands, turned, m_out, e_out):
    offsets_ref, coef_ref, slope_ref, base_ref = operands
    beams, bins = e_out.shape[1:]
    fine_bin = lax.broadcasted_iota(jnp.int32, (beams, LANES), 1)
    coarse_bin = fine_bin * LANES + first_bin
    rows = lax.broadcasted_iota(jnp.int32, (beams, 2 * beams), 0)
    lag = rows - offsets_ref[s, q : q + 1, :]
    matrix = jnp.zeros((beams, 2 * beams), jnp.float32)
    for t in range(coef_ref.shape[2]):
        matrix += jnp.where(lag == t, coef_ref[s, q, t : t + 1, :], 0.0)
    pad = jnp.zeros((beams - 2, 2 * beams), jnp.float32)
    stacked = jnp.concatenate([matrix, slope_ref[s, q : q + 1, :], base_ref[s, q : q + 1, :], pad], 0)
    turned[...] = stacked.T
    mine = turned[pl.ds(start, beams), :]
    high, low = split(mine[:, :beams])
    m_out[...] = jnp.concatenate([high, low, high], 1)
    slope = mine[:, beams : beams + 1]
    base = mine[:, beams + 1 : beams + 2]
    fine_cos, fine_sin = turn(slope * (fine_bin.astype(jnp.float32) / total))
    coarse_cos, coarse_sin = turn(slope * (coarse_bin.astype(jnp.float32) / total) + base)
    for k in range(bins // LANES):
        c, d = coarse_cos[:, k : k + 1], coarse_sin[:, k : k + 1]
        at = slice(k * LANES, (k + 1) * LANES)
        e_out[0, :, at] = c * fine_cos - d * fine_sin
        e_out[1, :, at] = d * fine_cos + c * fine_sin


def table_kernel(s, level, *refs):
    *operands, m_ref, e_ref, turned = refs
    beams, bins = e_ref.shape[2:]
    first_bin = lax.axis_index("tile") * bins
    total = float(bins * lax.axis_size("tile"))
    upper = (lax.axis_index("aperture") >> (level + s)) & 1
    start = pl.multiple_of(upper * beams, beams)
    for q in range(2):
        side = jnp.where(upper == q, 0, 1)
        side_table(s, q, start, first_bin, total, operands, turned, m_ref.at[side], e_ref.at[side])


def cross_table_kernel(level, first, bins, *refs):
    *operands, m_ref, e_ref, turned = refs
    beams = e_ref.shape[2]
    first_bin = lax.axis_index("tile") * bins + first
    total = float(bins * lax.axis_size("tile"))
    upper = (lax.axis_index("aperture") >> level) & 1
    start = pl.multiple_of((1 - upper) * beams, beams)
    for q in range(2):

        @pl.when(upper == q)
        def _(q=q):
            side_table(0, q, start, first_bin, total, operands, turned, m_ref.at[0], e_ref.at[0])


def focus_kernel(first, cuts, raw, far, near, w, steering, *refs):
    x = refs[-1]
    pulses, guards = raw.shape[1], near.shape[1]
    width = w.shape[1] // 2
    rows = pulses + guards
    blocks = x.shape[0] // rows - 1
    outs = refs[-1 - 2 * len(cuts) : -1]
    ahead = refs[: len(refs) - 1 - len(outs)] if first + blocks * width < raw.shape[2] else ()
    device = lax.axis_index("aperture")
    even = device % 2 == 0
    followed = device < lax.axis_size("aperture") - 1
    inner = lax.axis_index("tile") < lax.axis_size("tile") - 1
    nought = jnp.zeros((), jnp.bfloat16)

    for b in range(blocks + 1):
        at = first + b * width
        for part in range(2):
            if at == raw.shape[2]:
                own = jnp.where(inner, refs[0][part], nought)
                other = jnp.where(inner & followed, refs[1][part], nought)
            else:
                own = raw[part, :, at : at + width]
                other = jnp.where(even, near[part, :, at : at + width], far[part, :, at : at + width])
                other = jnp.where(followed, other, nought)
            lanes = slice(part * width, (part + 1) * width)
            x[b * rows : b * rows + pulses, lanes] = own
            x[b * rows + pulses : (b + 1) * rows, lanes] = other
    turned = jnp.concatenate([steering[0], steering[1]], 0)
    crossed = jnp.concatenate([-steering[1], steering[0]], 0)
    beams = steering.shape[1]
    out = jnp.dot(x[: blocks * rows], w[0], preferred_element_type=jnp.float32)
    out += jnp.dot(x[rows:], w[1], preferred_element_type=jnp.float32)
    out = out.astype(jnp.bfloat16)
    places = [(n, at) for n, size in enumerate(cuts) for at in range(0, size, LANES)]
    if ahead:
        places = places[ahead[0].shape[2] // LANES :]
        for ref, value in zip(outs, ahead):
            ref[:, :, : value.shape[2]] = value[...]
    for b in range(blocks):
        re = out[b * rows : (b + 1) * rows, :width]
        im = out[b * rows : (b + 1) * rows, width:]
        sub = jnp.dot(turned, re, preferred_element_type=jnp.float32)
        sub += jnp.dot(crossed, im, preferred_element_type=jnp.float32)
        for k in range(width // LANES):
            n, at = places[b * (width // LANES) + k]
            for ref, value in zip(outs[2 * n : 2 * n + 2], split(sub[:, k * LANES : (k + 1) * LANES])):
                ref[0, :, at : at + LANES] = value[:beams]
                ref[1, :, at : at + LANES] = value[beams:]


def split_parts(values):
    high, low = zip(*[split(value) for value in values])
    return high, low


def turned_term(first, side, given, m, e):
    bins = given[0][0].shape[1]
    beams = m.shape[1]
    at = slice(first, first + bins)
    terms = []
    for part in range(2):
        high = given[0][part]
        stacked = [high, high] + ([given[1][part]] if len(given) > 1 else [])
        weights = m[side][:, : len(stacked) * beams]
        stacked = jnp.concatenate(stacked, 0)
        terms.append(jnp.dot(weights, stacked, preferred_element_type=jnp.float32))
    c, d = e[side, 0, :, at], e[side, 1, :, at]
    return c * terms[0] - d * terms[1], d * terms[0] + c * terms[1]


def turned_sum(first, own, other, m, e):
    left, right = turned_term(first, 0, own, m, e), turned_term(first, 1, other, m, e)
    return left[0] + right[0], left[1] + right[1]


def store_split(values, high_ref, low_ref):
    for part, value in enumerate(values):
        high_ref[part], low_ref[part] = split(value)


def first_merge_kernel(first, high, low, other, m, e, high_ref, low_ref):
    store_split(turned_sum(first, (high, low), (other,), m, e), high_ref, low_ref)


def write_image(values, first, image, held, sem):
    copies = []
    for part, value in enumerate(values):
        held[part] = value
        place = image.at[part, :, first : first + held.shape[2]]
        copies.append(pltpu.make_async_copy(held.at[part], place, sem.at[part]))
        copies[-1].start()
    return copies


def start_image_kernel(first, high, low, other, m, e, image, held, sem):
    for copy in write_image(turned_sum(first, (high, low), (other,), m, e), first, image, held, sem):
        copy.wait()


def own_term_kernel(first, high, low, m, e, out):
    out[0], out[1] = turned_term(first, 0, (high, low), m, e)


def both_terms_kernel(first, place, high, low, over, m0, e0, m1, e1, out):
    own, other = [split_parts(turned_term(place, 0, parts, m0, e0)) for parts in ((high, low), (over,))]
    for part, value in enumerate(turned_sum(first, own, other, m1, e1)):
        out[part] = value.astype(out.dtype)


def end_image_kernel(first, first_out, own, other, m, e, out, got, _, image, held, held_out, sem):
    values = [out[part] + got[part].astype(jnp.float32) for part in range(2)]
    copies = write_image(values, first_out, image, held_out, sem.at[2:4])
    term = turned_term(first, 1, (other,), m, e)
    copies += write_image((own[0] + term[0], own[1] + term[1]), first, image, held, sem)
    for copy in copies:
        copy.wait()


def cut_kernel(raw, guard, rim, corner, sem):
    guards, width = corner.shape[1:]
    copies = [
        pltpu.make_async_copy(raw.at[:, :guards, :], guard, sem.at[0]),
        pltpu.make_async_copy(raw.at[:, :, :width], rim, sem.at[1]),
        pltpu.make_async_copy(raw.at[:, :guards, :width], corner, sem.at[2]),
    ]
    for copy in copies:
        copy.start()
    for copy in copies:
        copy.wait()


def shards(raw, taps, steering, offsets, coef, slope, base):
    pulses, bins = raw.shape[1:]
    width = taps.shape[1]
    beams = steering.shape[1]
    guards = steering.shape[2] - pulses
    count, tiles = lax.axis_size("aperture"), lax.axis_size("tile")
    level = count.bit_length() - 3
    bf16, f32 = jnp.bfloat16, jnp.float32
    sds = jax.ShapeDtypeStruct
    anywhere = pl.BlockSpec(memory_space=pl.ANY)
    whole = pl.BlockSpec(memory_space=pltpu.VMEM)

    guard, rim, corner = call(
        cut_kernel,
        [sds((2, guards, bins), bf16), sds((2, pulses, width), bf16), sds((2, guards, width), bf16)],
        [raw],
        scratch=[pltpu.SemaphoreType.DMA((3,))],
        in_specs=[pl.BlockSpec(memory_space=pltpu.HBM)],
        out_specs=[anywhere] * 3,
    )
    near = lax.ppermute(guard, "aperture", completed([(d, d - 1) for d in range(1, count, 2)], count))
    spare = {d: d - 1 if d % 4 == 3 else d + 3 for d in range(1, count, 2) if d % 4 == 3 or d + 3 < count}
    far = lax.ppermute(guard, "aperture", completed([(d, d - 1) for d in range(2, count, 2)], count, spare))
    rim = lax.ppermute(rim, "tile", completed([(t, t - 1) for t in range(1, tiles)], tiles))
    steps = [(d * tiles + t, (d - 1) * tiles + t - 1) for d in range(1, count) for t in range(1, tiles)]
    corner = lax.ppermute(corner, ("aperture", "tile"), completed(steps, count * tiles))
    w = call(toeplitz_kernel, sds((2, 2 * width, 2 * width), bf16), [taps])
    def tables(body, sides, size, after=()):
        return call(
            body,
            [sds((sides, beams, 3 * beams), bf16), sds((sides, 2, beams, size), f32)],
            [offsets, jnp.swapaxes(coef, 2, 3), slope, base],
            scratch=[pltpu.VMEM((2 * beams, 2 * beams), f32)],
            flops=20_000_000,
            after=after,
        )

    first_tables = tables(functools.partial(table_kernel, 0, level), 2, bins)

    def partner(value, bit):
        return lax.ppermute(value, "aperture", [(d, d ^ (1 << bit)) for d in range(count)])

    def focus(first, cuts, blocks, after, more=(), flops=0):
        rows = pulses + guards
        return call(
            functools.partial(focus_kernel, first, cuts),
            [sds((2, beams, size), bf16) for size in cuts for _ in range(2)],
            [raw, far, near, w, steering, *more],
            scratch=[pltpu.VMEM(((blocks + 1) * rows, 2 * width), bf16)],
            flops=flops,
            after=[after],
        )

    def first_merge(first, sub, other, after, flops=0):
        shape = sds(other.shape, bf16)
        return call(
            functools.partial(first_merge_kernel, first),
            [shape, shape],
            [*sub, other, *first_tables],
            flops=flops,
            after=after,
        )

    def write(body, sizes, args, image=None):
        given = [] if image is None else [image]
        return call(
            body,
            sds((2, beams, bins), f32),
            [*args, *given],
            scratch=[*[pltpu.VMEM((2, beams, size), f32) for size in sizes], pltpu.SemaphoreType.DMA((4,))],
            aliases={len(args): 0} if given else {},
            in_specs=[whole] * len(args) + [anywhere] * len(given),
            out_specs=anywhere,
            flops=0 if given else WAIT,
        )

    assert bins >= 4 * width and bins % width == 0
    middle, last = width + LANES, bins - width
    *sub, high, low = focus(0, [middle, 2 * width - middle], 2, first_tables[0])
    crossing = focus(2 * width, [last - middle], (last - 2 * width) // width, sub[0], [high, low])
    last_sub = focus(last, [width], 1, crossing[0], [rim, corner], WAIT)
    other = partner(sub[0], level)
    over = partner(crossing[0], level + 1)
    last_other = partner(last_sub[0], level)
    second = first_merge(0, sub, other, [last_sub[0]], WAIT)
    third = partner(second[0], level + 1)
    last_tables = tables(functools.partial(table_kernel, 1, level), 2, bins, [second[0]])
    cross = tables(functools.partial(cross_table_kernel, level, middle, bins), 1, last - middle, [second[0]])
    last_second = first_merge(last, last_sub, last_other, [last_tables[0], cross[0]], WAIT)
    last_third = partner(last_second[0], level + 1)
    def both_terms(place, used, dtype, after):
        return call(
            functools.partial(both_terms_kernel, middle, place),
            sds((2, beams, last - middle), dtype),
            [*crossing, over, *used, *last_tables],
            after=[after],
        )

    sent = both_terms(0, cross, bf16, last_second[0])
    got = partner(sent, level)
    out = both_terms(middle, first_tables, f32, sent)
    image = write(functools.partial(start_image_kernel, 0), [middle], [*second, third, *last_tables])
    own = call(
        functools.partial(own_term_kernel, last),
        sds((2, beams, width), f32),
        [*last_second, *last_tables],
        after=[sent],
    )
    return write(
        functools.partial(end_image_kernel, last, middle),
        [width, last - middle],
        [own, last_third, *last_tables, out, got],
        image,
    )


def solution(mesh):
    placed = (P(None, "aperture", "tile"), P(), P(), P(), P(), P(), P())
    return jax.shard_map(
        shards, mesh=mesh, in_specs=placed, out_specs=P(None, "aperture", "tile"), check_vma=False
    )
```

```python
import functools
import math

import jax
import jax.numpy as jnp
from jax import lax
from jax.experimental import pallas as pl
from jax.experimental.pallas import tpu as pltpu
from jax.sharding import PartitionSpec as P

LANES = 128
WAIT = 2_000_000_000
VMEM = pltpu.CompilerParams(vmem_limit_bytes=12 * 1024 * 1024)


def call(body, outs, args, scratch=(), flops=0, aliases=None, in_specs=None, out_specs=None, after=()):
    whole = pl.BlockSpec(memory_space=pltpu.VMEM)
    if after:
        inner, given, unused = body, len(args), len(after)
        in_specs = (in_specs or [whole] * given) + [pl.BlockSpec(memory_space=pl.ANY)] * unused
        args = list(args) + list(after)

        def body(*refs):
            inner(*refs[:given], *refs[given + unused :])

    many = isinstance(outs, (list, tuple))
    return pl.pallas_call(
        body,
        out_shape=outs,
        in_specs=in_specs or [whole] * len(args),
        out_specs=out_specs or ([whole] * len(outs) if many else whole),
        scratch_shapes=list(scratch),
        input_output_aliases=aliases or {},
        compiler_params=VMEM,
        cost_estimate=pl.CostEstimate(flops=flops, bytes_accessed=0, transcendentals=0),
    )(*args)


def completed(pairs, count, spare=None):
    needed = dict(pairs)
    if spare is None:
        spare = {t: s for s, t in needed.items()}
    taken = set(needed.values())
    moves = {**needed, **{s: t for s, t in spare.items() if s not in needed and t not in taken}}
    sources = [d for d in range(count) if d not in moves]
    targets = [d for d in range(count) if d not in moves.values()]
    for d in [d for d in sources if d in targets]:
        ways = [(abs(s - d) + abs(t - d), s) for s, t in moves.items() if needed.get(s) != t]
        start = min(ways)[1] if ways else d
        moves[d] = moves.get(start, d)
        moves[start] = d
    moves.update(zip([d for d in sources if d not in moves], [d for d in targets if d not in moves.values()]))
    return sorted(moves.items())


def toeplitz_kernel(taps_ref, w_ref):
    count = taps_ref.shape[1]
    halves = []
    taps = taps_ref[...].astype(jnp.float32)
    for part in range(2):
        row = taps[part : part + 1, :]
        row = jnp.concatenate([row, jnp.zeros_like(row)], 1)
        rows = jnp.broadcast_to(row, (count, 2 * count))
        rolled = pltpu.roll(rows, 0, 1, stride=1, stride_axis=0)
        halves.append(rolled.T)
    for side in range(2):
        re = halves[0][side * count : (side + 1) * count].astype(jnp.bfloat16)
        im = halves[1][side * count : (side + 1) * count].astype(jnp.bfloat16)
        w_ref[side, :count, :count] = re
        w_ref[side, :count, count:] = -im
        w_ref[side, count:, :count] = im
        w_ref[side, count:, count:] = re


def split(value):
    high = value.astype(jnp.bfloat16)
    low = (value - high.astype(jnp.float32)).astype(jnp.bfloat16)
    return high, low


def turn(angle):
    quarters = jnp.floor(angle * (2 / math.pi) + 0.5)
    rest = angle - quarters * 1.5703125
    rest = rest - quarters * 4.837512969970703125e-4
    rest = rest - quarters * 7.54978995489188216e-8
    z = rest * rest
    sine = rest + rest * z * (-1.6666654611e-1 + z * (8.3321608736e-3 - z * 1.9515295891e-4))
    cosine = 1 - 0.5 * z + z * z * (
        4.166664568298827e-2 + z * (-1.388731625493765e-3 + z * 2.443315711809948e-5)
    )
    which = quarters.astype(jnp.int32)
    odd = (which & 1) == 1
    c, d = jnp.where(odd, sine, cosine), jnp.where(odd, cosine, sine)
    c = jnp.where(((which + 1) & 2) == 2, -c, c)
    d = jnp.where((which & 2) == 2, -d, d)
    return c, d


def side_table(s, q, start, first_bin, total, operands, turned, m_out, e_out):
    offsets_ref, coef_ref, slope_ref, base_ref = operands
    beams, bins = e_out.shape[1:]
    fine_bin = lax.broadcasted_iota(jnp.int32, (beams, LANES), 1)
    coarse_bin = fine_bin * LANES + first_bin
    rows = lax.broadcasted_iota(jnp.int32, (beams, 2 * beams), 0)
    lag = rows - offsets_ref[s, q : q + 1, :]
    matrix = jnp.zeros((beams, 2 * beams), jnp.float32)
    for t in range(coef_ref.shape[2]):
        matrix += jnp.where(lag == t, coef_ref[s, q, t : t + 1, :], 0.0)
    pad = jnp.zeros((beams - 2, 2 * beams), jnp.float32)
    stacked = jnp.concatenate([matrix, slope_ref[s, q : q + 1, :], base_ref[s, q : q + 1, :], pad], 0)
    turned[...] = stacked.T
    mine = turned[pl.ds(start, beams), :]
    high, low = split(mine[:, :beams])
    m_out[...] = jnp.concatenate([high, low, high], 1)
    slope = mine[:, beams : beams + 1]
    base = mine[:, beams + 1 : beams + 2]
    fine_cos, fine_sin = turn(slope * (fine_bin.astype(jnp.float32) / total))
    coarse_cos, coarse_sin = turn(slope * (coarse_bin.astype(jnp.float32) / total) + base)
    for k in range(bins // LANES):
        c, d = coarse_cos[:, k : k + 1], coarse_sin[:, k : k + 1]
        at = slice(k * LANES, (k + 1) * LANES)
        e_out[0, :, at] = c * fine_cos - d * fine_sin
        e_out[1, :, at] = d * fine_cos + c * fine_sin


def table_kernel(s, level, *refs):
    *operands, m_ref, e_ref, turned = refs
    beams, bins = e_ref.shape[2:]
    first_bin = lax.axis_index("tile") * bins
    total = float(bins * lax.axis_size("tile"))
    upper = (lax.axis_index("aperture") >> (level + s)) & 1
    start = pl.multiple_of(upper * beams, beams)
    for q in range(2):
        side = jnp.where(upper == q, 0, 1)
        side_table(s, q, start, first_bin, total, operands, turned, m_ref.at[side], e_ref.at[side])


def cross_table_kernel(level, first, bins, *refs):
    *operands, m_ref, e_ref, turned = refs
    beams = e_ref.shape[2]
    first_bin = lax.axis_index("tile") * bins + first
    total = float(bins * lax.axis_size("tile"))
    upper = (lax.axis_index("aperture") >> level) & 1
    start = pl.multiple_of((1 - upper) * beams, beams)
    for q in range(2):

        @pl.when(upper == q)
        def _(q=q):
            side_table(0, q, start, first_bin, total, operands, turned, m_ref.at[0], e_ref.at[0])


def focus_kernel(first, cuts, raw, far, near, w, steering, *refs):
    x = refs[-1]
    pulses, guards = raw.shape[1], near.shape[1]
    width = w.shape[1] // 2
    rows = pulses + guards
    blocks = x.shape[0] // rows - 1
    outs = refs[-1 - 2 * len(cuts) : -1]
    ahead = refs[: len(refs) - 1 - len(outs)] if first + blocks * width < raw.shape[2] else ()
    device = lax.axis_index("aperture")
    even = device % 2 == 0
    followed = device < lax.axis_size("aperture") - 1
    inner = lax.axis_index("tile") < lax.axis_size("tile") - 1
    nought = jnp.zeros((), jnp.bfloat16)

    for b in range(blocks + 1):
        at = first + b * width
        for part in range(2):
            if at == raw.shape[2]:
                own = jnp.where(inner, refs[0][part], nought)
                other = jnp.where(inner & followed, refs[1][part], nought)
            else:
                own = raw[part, :, at : at + width]
                other = jnp.where(even, near[part, :, at : at + width], far[part, :, at : at + width])
                other = jnp.where(followed, other, nought)
            lanes = slice(part * width, (part + 1) * width)
            x[b * rows : b * rows + pulses, lanes] = own
            x[b * rows + pulses : (b + 1) * rows, lanes] = other
    turned = jnp.concatenate([steering[0], steering[1]], 0)
    crossed = jnp.concatenate([-steering[1], steering[0]], 0)
    beams = steering.shape[1]
    out = jnp.dot(x[: blocks * rows], w[0], preferred_element_type=jnp.float32)
    out += jnp.dot(x[rows:], w[1], preferred_element_type=jnp.float32)
    out = out.astype(jnp.bfloat16)
    places = [(n, at) for n, size in enumerate(cuts) for at in range(0, size, LANES)]
    if ahead:
        places = places[ahead[0].shape[2] // LANES :]
        for ref, value in zip(outs, ahead):
            ref[:, :, : value.shape[2]] = value[...]
    for b in range(blocks):
        re = out[b * rows : (b + 1) * rows, :width]
        im = out[b * rows : (b + 1) * rows, width:]
        sub = jnp.dot(turned, re, preferred_element_type=jnp.float32)
        sub += jnp.dot(crossed, im, preferred_element_type=jnp.float32)
        for k in range(width // LANES):
            n, at = places[b * (width // LANES) + k]
            for ref, value in zip(outs[2 * n : 2 * n + 2], split(sub[:, k * LANES : (k + 1) * LANES])):
                ref[0, :, at : at + LANES] = value[:beams]
                ref[1, :, at : at + LANES] = value[beams:]


def split_parts(values):
    high, low = zip(*[split(value) for value in values])
    return high, low


def turned_term(first, side, given, m, e):
    bins = given[0][0].shape[1]
    beams = m.shape[1]
    at = slice(first, first + bins)
    terms = []
    for part in range(2):
        high = given[0][part]
        stacked = [high, high] + ([given[1][part]] if len(given) > 1 else [])
        weights = m[side][:, : len(stacked) * beams]
        stacked = jnp.concatenate(stacked, 0)
        terms.append(jnp.dot(weights, stacked, preferred_element_type=jnp.float32))
    c, d = e[side, 0, :, at], e[side, 1, :, at]
    return c * terms[0] - d * terms[1], d * terms[0] + c * terms[1]


def turned_sum(first, own, other, m, e):
    left, right = turned_term(first, 0, own, m, e), turned_term(first, 1, other, m, e)
    return left[0] + right[0], left[1] + right[1]


def store_split(values, high_ref, low_ref):
    for part, value in enumerate(values):
        high_ref[part], low_ref[part] = split(value)


def first_merge_kernel(first, high, low, other, m, e, high_ref, low_ref):
    store_split(turned_sum(first, (high, low), (other,), m, e), high_ref, low_ref)


def write_image(values, first, image, held, sem):
    copies = []
    for part, value in enumerate(values):
        held[part] = value
        place = image.at[part, :, first : first + held.shape[2]]
        copies.append(pltpu.make_async_copy(held.at[part], place, sem.at[part]))
        copies[-1].start()
    return copies


def start_image_kernel(first, high, low, other, m, e, image, held, sem):
    for copy in write_image(turned_sum(first, (high, low), (other,), m, e), first, image, held, sem):
        copy.wait()


def own_term_kernel(first, high, low, m, e, out):
    out[0], out[1] = turned_term(first, 0, (high, low), m, e)


def both_terms_kernel(first, place, high, low, over, m0, e0, m1, e1, out):
    own, other = [split_parts(turned_term(place, 0, parts, m0, e0)) for parts in ((high, low), (over,))]
    for part, value in enumerate(turned_sum(first, own, other, m1, e1)):
        out[part] = value.astype(out.dtype)


def next_image_kernel(first, own, other, m, e, _, image, held, sem):
    term = turned_term(first, 1, (other,), m, e)
    for copy in write_image((own[0] + term[0], own[1] + term[1]), first, image, held, sem):
        copy.wait()


def end_image_kernel(first, out, got, _, image, held, sem):
    values = [out[part] + got[part].astype(jnp.float32) for part in range(2)]
    for copy in write_image(values, first, image, held, sem):
        copy.wait()


def cut_kernel(raw, guard, rim, corner, sem):
    guards, width = corner.shape[1:]
    copies = [
        pltpu.make_async_copy(raw.at[:, :guards, :], guard, sem.at[0]),
        pltpu.make_async_copy(raw.at[:, :, :width], rim, sem.at[1]),
        pltpu.make_async_copy(raw.at[:, :guards, :width], corner, sem.at[2]),
    ]
    for copy in copies:
        copy.start()
    for copy in copies:
        copy.wait()


def shards(raw, taps, steering, offsets, coef, slope, base):
    pulses, bins = raw.shape[1:]
    width = taps.shape[1]
    beams = steering.shape[1]
    guards = steering.shape[2] - pulses
    count, tiles = lax.axis_size("aperture"), lax.axis_size("tile")
    level = count.bit_length() - 3
    bf16, f32 = jnp.bfloat16, jnp.float32
    sds = jax.ShapeDtypeStruct
    anywhere = pl.BlockSpec(memory_space=pl.ANY)
    whole = pl.BlockSpec(memory_space=pltpu.VMEM)

    guard, rim, corner = call(
        cut_kernel,
        [sds((2, guards, bins), bf16), sds((2, pulses, width), bf16), sds((2, guards, width), bf16)],
        [raw],
        scratch=[pltpu.SemaphoreType.DMA((3,))],
        in_specs=[pl.BlockSpec(memory_space=pltpu.HBM)],
        out_specs=[anywhere] * 3,
    )
    near = lax.ppermute(guard, "aperture", completed([(d, d - 1) for d in range(1, count, 2)], count))
    spare = {d: d - 1 if d % 4 == 3 else d + 3 for d in range(1, count, 2) if d % 4 == 3 or d + 3 < count}
    far = lax.ppermute(guard, "aperture", completed([(d, d - 1) for d in range(2, count, 2)], count, spare))
    rim = lax.ppermute(rim, "tile", completed([(t, t - 1) for t in range(1, tiles)], tiles))
    steps = [(d * tiles + t, (d - 1) * tiles + t - 1) for d in range(1, count) for t in range(1, tiles)]
    corner = lax.ppermute(corner, ("aperture", "tile"), completed(steps, count * tiles))
    w = call(toeplitz_kernel, sds((2, 2 * width, 2 * width), bf16), [taps])
    def tables(body, sides, size, after=()):
        return call(
            body,
            [sds((sides, beams, 3 * beams), bf16), sds((sides, 2, beams, size), f32)],
            [offsets, jnp.swapaxes(coef, 2, 3), slope, base],
            scratch=[pltpu.VMEM((2 * beams, 2 * beams), f32)],
            flops=20_000_000,
            after=after,
        )

    first_tables = tables(functools.partial(table_kernel, 0, level), 2, bins)

    def partner(value, bit):
        return lax.ppermute(value, "aperture", [(d, d ^ (1 << bit)) for d in range(count)])

    def focus(first, cuts, blocks, after, more=(), flops=0):
        rows = pulses + guards
        return call(
            functools.partial(focus_kernel, first, cuts),
            [sds((2, beams, size), bf16) for size in cuts for _ in range(2)],
            [raw, far, near, w, steering, *more],
            scratch=[pltpu.VMEM(((blocks + 1) * rows, 2 * width), bf16)],
            flops=flops,
            after=[after],
        )

    def first_merge(first, sub, other, after, flops=0):
        shape = sds(other.shape, bf16)
        return call(
            functools.partial(first_merge_kernel, first),
            [shape, shape],
            [*sub, other, *first_tables],
            flops=flops,
            after=after,
        )

    def write(body, size, args, image=None):
        given = [] if image is None else [image]
        return call(
            body,
            sds((2, beams, bins), f32),
            [*args, *given],
            scratch=[pltpu.VMEM((2, beams, size), f32), pltpu.SemaphoreType.DMA((2,))],
            aliases={len(args): 0} if given else {},
            in_specs=[whole] * len(args) + [anywhere] * len(given),
            out_specs=anywhere,
            flops=0 if given else WAIT,
        )

    assert bins >= 4 * width and bins % width == 0
    middle, last = width + LANES, bins - width
    *sub, high, low = focus(0, [middle, 2 * width - middle], 2, first_tables[0])
    crossing = focus(2 * width, [last - middle], (last - 2 * width) // width, sub[0], [high, low])
    last_sub = focus(last, [width], 1, crossing[0], [rim, corner], WAIT)
    other = partner(sub[0], level)
    over = partner(crossing[0], level + 1)
    last_other = partner(last_sub[0], level)
    second = first_merge(0, sub, other, [last_sub[0]], WAIT)
    third = partner(second[0], level + 1)
    last_tables = tables(functools.partial(table_kernel, 1, level), 2, bins, [second[0]])
    cross = tables(functools.partial(cross_table_kernel, level, middle, bins), 1, last - middle, [second[0]])
    last_second = first_merge(last, last_sub, last_other, [last_tables[0], cross[0]], WAIT)
    last_third = partner(last_second[0], level + 1)
    def both_terms(place, used, dtype, after):
        return call(
            functools.partial(both_terms_kernel, middle, place),
            sds((2, beams, last - middle), dtype),
            [*crossing, over, *used, *last_tables],
            after=[after],
        )

    sent = both_terms(0, cross, bf16, last_second[0])
    got = partner(sent, level)
    out = both_terms(middle, first_tables, f32, sent)
    image = write(functools.partial(start_image_kernel, 0), middle, [*second, third, *last_tables])
    own = call(
        functools.partial(own_term_kernel, last),
        sds((2, beams, width), f32),
        [*last_second, *last_tables],
        after=[sent],
    )
    image = write(
        functools.partial(next_image_kernel, last), width, [own, last_third, *last_tables], image
    )
    return write(functools.partial(end_image_kernel, middle), last - middle, [out, got], image)


def solution(mesh):
    placed = (P(None, "aperture", "tile"), P(), P(), P(), P(), P(), P())
    return jax.shard_map(
        shards, mesh=mesh, in_specs=placed, out_specs=P(None, "aperture", "tile"), check_vma=False
    )
```
